256 devices in a mesh: row: 8 (over z), col: 32 (over x, y, core).
Axes of the slice: x: 4, y: 4, z: 8, core: 2. Of those that a mesh axis runs over, the one named last changes fastest.
Arguments:
- diag_tile: float32 [2048, 2048], P(('row', 'col')), as said below
- row_pan_u: float32 [8, 64, 2048], P('row', 'col'), may hold values from -6 to 6
- row_pan_v: float32 [8, 64, 2048], P('row', 'col'), may hold values from -0.5 to 0.5
- col_pan_u: float32 [32, 64, 2048], P('col', 'row'), may hold values from -6 to 6
- col_pan_v: float32 [32, 64, 2048], P('col', 'row'), may hold values from -0.5 to 0.5
- trail_u: float32 [8, 32, 64, 2048], P('row', 'col'), may hold values from -6 to 6
- trail_v: float32 [8, 32, 64, 2048], P('row', 'col'), may hold values from -6 to 6
Outputs:
- diag_factor: float32 [2048, 2048], P(('row', 'col'))
- row_solved: float32 [8, 64, 2048], P('row', 'col')
- col_solved: float32 [32, 64, 2048], P('col', 'row')
- grown_u: float32 [8, 32, 128, 2048], P('row', 'col')
- grown_v: float32 [8, 32, 128, 2048], P('row', 'col')
The draws below stay inside these ranges and needn't reach their ends.
Inputs may be any that keep to these rules, and one draw needn't show every extreme that they name: `diag_tile`: symmetric positive definite: an exponential covariance of 2048 jittered sites on a grid, plus the identity.
All inputs are finite; a program needn't handle non-finite values.
Results may differ from the reference program's by a relative error of at most 0.0003.
Values sent between devices are 32-bit elements; how exact they have to be, the bound alone decides.
No kernel may reach another device: no remote copies, remote signals or barrier semaphores. Data moves between devices by JAX's collectives and lax.ppermute only.
A program may use at most 128 MiB of HBM per device.

```python
import math
import jax
import jax.numpy as jnp
from jax import lax

B = 2048
R = 64
NR = 8
NC = 32


def curve_cells(count):
    index = jnp.arange(count, dtype=jnp.int32)
    grid_x = jnp.zeros((count,), jnp.int32)
    grid_y = jnp.zeros((count,), jnp.int32)
    for level in range(8):
        grid_x = grid_x + index // 4 ** level % 2 * 2 ** level
        grid_y = grid_y + index // (2 * 4 ** level) % 2 * 2 ** level
    return (grid_x.astype(jnp.float32), grid_y.astype(jnp.float32))


def draw_diag_tile(key, part):
    key = jax.random.fold_in(key, 7)
    key_sites, key_scale = jax.random.split(key, 2)
    grid_x, grid_y = curve_cells(B)
    extent = math.sqrt(B)
    jitter = jax.random.uniform(key_sites, (2, B), minval=0.2, maxval=0.8)
    scales = jnp.exp(jax.random.uniform(key_scale, (B,), minval=-0.7, maxval=0.7))
    length = 0.5 * extent
    places_x = grid_x + jitter[0]
    places_y = grid_y + jitter[1]
    apart_x = places_x[:, None] - places_x[None, :]
    apart_y = places_y[:, None] - places_y[None, :]
    distance = jnp.sqrt(apart_x * apart_x + apart_y * apart_y)
    covariance = scales[:, None] * scales[None, :] * jnp.exp(-distance / length)
    return covariance + jnp.eye(B, dtype=jnp.float32)


def steps_of(key, shape, cuts, smallest, high):
    loudness, own = 1.0, jax.random.fold_in(key, 6)
    for position, parts in cuts:
        draws = jnp.exp(jax.random.uniform(jax.random.fold_in(own, position), (parts,), jnp.float32, smallest / len(cuts), high / len(cuts)))
        loudness = loudness * jnp.repeat(draws, shape[position] // parts).reshape([-1 if axis == position else 1 for axis in range(len(shape))])
    return loudness


def gaussian(own_key, shape, scale, most, shards=(), kind=jnp.bfloat16):
    drawn = jax.random.normal(own_key, shape, jnp.float32) * scale
    if len(shards) > 0:
        drawn = steps_of(own_key, shape, shards, -0.22, 0.18) * drawn
    return jnp.clip(drawn, min=-most, max=most).astype(kind)


def setup_inputs(seed: int = 0) -> dict:
    streams_of = jax.random.split(jax.random.key(seed), 8)
    diag_tile = draw_diag_tile(jax.random.fold_in(streams_of[7], 71), 0)
    row_pan_u = gaussian(streams_of[1], (NR, R, B), 1.0, 6.0, ((0, 8), (1, 32)), jnp.float32)
    row_pan_v = gaussian(streams_of[2], (NR, R, B), 0.08, 0.5, ((0, 8), (1, 32)), jnp.float32)
    col_pan_u = gaussian(streams_of[3], (NC, R, B), 1.0, 6.0, ((0, 32), (1, 8)), jnp.float32)
    col_pan_v = gaussian(streams_of[4], (NC, R, B), 0.08, 0.5, ((0, 32), (1, 8)), jnp.float32)
    trail_u = gaussian(streams_of[5], (NR, NC, R, B), 1.0, 6.0, ((0, 8), (1, 32)), jnp.float32)
    trail_v = gaussian(streams_of[6], (NR, NC, R, B), 1.0, 6.0, ((0, 8), (1, 32)), jnp.float32)
    return {"diag_tile": diag_tile, "row_pan_u": row_pan_u, "row_pan_v": row_pan_v, "col_pan_u": col_pan_u, "col_pan_v": col_pan_v, "trail_u": trail_u, "trail_v": trail_v}


def solve_panel(factor, panel):
    count = panel.shape[0]
    width = panel.shape[1]
    stacked = jnp.transpose(panel, (2, 0, 1)).reshape(B, count * width)
    solved = lax.linalg.triangular_solve(factor, stacked, left_side=True, lower=True)
    return jnp.transpose(solved.reshape(B, count, width), (1, 2, 0))

def reference(diag_tile, row_pan_u, row_pan_v, col_pan_u, col_pan_v, trail_u, trail_v):
    factor = jnp.linalg.cholesky(diag_tile)
    row_solved = solve_panel(factor, row_pan_v)
    col_solved = solve_panel(factor, col_pan_v)
    coupling = jnp.einsum('arx,bsx->abrs', row_solved, col_solved, precision=lax.Precision.HIGHEST)
    update = -jnp.einsum('abrs,arx->absx', coupling, row_pan_u, precision=lax.Precision.HIGHEST)
    grown_u = jnp.concatenate([trail_u, update], axis=2)
    spread = jnp.broadcast_to(col_pan_u[None], trail_v.shape)
    grown_v = jnp.concatenate([trail_v, spread], axis=2)
    return (factor, row_solved, col_solved, grown_u, grown_v)
```

```python
import jax
import jax.numpy as jnp
from jax import lax
from jax.experimental import pallas as pl
from jax.experimental.pallas import tpu as pltpu
from jax.sharding import PartitionSpec as P

F32 = jnp.float32
BF16 = jnp.bfloat16
SIZE = 2048
PANEL = 256
COUNT = SIZE // PANEL
HALF = PANEL // 2
RANK = 64
NT = (((1,), (1,)), ((), ()))
TN = (((0,), (0,)), ((), ()))
NN = (((1,), (0,)), ((), ()))


def exact(left, right, dims):
    return lax.dot_general(left, right, dims, precision=lax.Precision.HIGHEST, preferred_element_type=F32)


def split(value):
    high = value.astype(BF16)
    return high, (value - high.astype(F32)).astype(BF16)


def iota(shape, dim):
    return lax.broadcasted_iota(jnp.int32, shape, dim)


def along_rows(value, row):
    return jnp.broadcast_to(value[row : row + 1, :], value.shape)


def along_lanes(value, lane):
    return jnp.broadcast_to(value[:, lane : lane + 1], value.shape)


def total(terms):
    while len(terms) > 1:
        terms = [
            terms[i] + terms[i + 1] if i + 1 < len(terms) else terms[i]
            for i in range(0, len(terms), 2)
        ]
    return terms[0]


def factor_block(block, groups=2):
    count = len(block)
    size = 8 * count
    width = 8 * groups
    work = list(block)
    sub = iota((8, size), 0)
    lane = iota((8, size), 1)
    side = [jnp.where(sub + 8 * i == lane, 1.0, 0.0).astype(F32) for i in range(count)]
    upper = [None] * count
    inverse = [None] * count
    for top in range(0, count, groups):
        rows = work[top : top + groups]
        eyes = side[top : top + groups]
        cols = [[along_lanes(rows[a], 8 * top + k) for a in range(groups)] for k in range(width)]
        below = {
            i: [along_lanes(work[i], 8 * top + k) for k in range(width)]
            for i in range(top + groups, count)
        }
        up = [jnp.zeros((8, size), F32)] * groups
        inv = [jnp.zeros((8, size), F32)] * groups
        for k in range(width):
            ka, ks = divmod(k, 8)
            pivot = along_rows(cols[k][ka], ks)
            scale = 1.0 / pivot
            root = lax.rsqrt(pivot)
            row_k = along_rows(rows[ka], ks)
            eye_k = along_rows(eyes[ka], ks)
            here = sub == ks
            up[ka] = jnp.where(here, row_k * root, up[ka])
            inv[ka] = jnp.where(here, eye_k * root, inv[ka])
            times = []
            for a in range(groups):
                ratio = cols[k][a] * scale
                times.append(jnp.where(here, 1.0 - scale, ratio) if a == ka else ratio)
            for a in range(groups):
                rows[a] = rows[a] - times[a] * row_k
                eyes[a] = eyes[a] - times[a] * eye_k
            for m in range(k + 1, width):
                col_m = along_rows(cols[m][ka], ks)
                cols[m] = [cols[m][a] - times[a] * col_m for a in range(groups)]
        upper[top : top + groups] = up
        inverse[top : top + groups] = inv
        row_all = [along_rows(rows[k // 8], k % 8) for k in range(width)]
        eye_all = [along_rows(eyes[k // 8], k % 8) for k in range(width)]
        for i in range(top + groups, count):
            work[i] = work[i] - total([below[i][k] * row_all[k] for k in range(width)])
            side[i] = side[i] - total([below[i][k] * eye_all[k] for k in range(width)])
    upper = [jnp.where(sub + 8 * i <= lane, upper[i], 0.0) for i in range(count)]
    inverse = [jnp.where(sub + 8 * i >= lane, inverse[i], 0.0) for i in range(count)]
    return jnp.concatenate(upper, axis=0), jnp.concatenate(inverse, axis=0)


def factor_values(value):
    return factor_block([value[8 * i : 8 * i + 8, :] for i in range(value.shape[0] // 8)])


def panel_kernel(
    place_ref, diag_ref, pan_ref, base_ref, trail_ref,
    own_ref, solved_ref, grown_ref,
    work, high, low, inverse, sems,
):
    own_tile = place_ref[0]
    own_row = pl.multiple_of(place_ref[1], 8)

    def fetch(k, slot):
        cols = pl.ds(pl.multiple_of(k * PANEL, PANEL), PANEL)
        return (
            pltpu.make_async_copy(diag_ref.at[:, cols], work.at[slot, pl.ds(0, SIZE)], sems.at[slot, 0]),
            pltpu.make_async_copy(pan_ref.at[:, cols], work.at[slot, pl.ds(SIZE, 2 * RANK)], sems.at[slot, 1]),
        )

    for copy in fetch(0, 0):
        copy.start()
    work[0, SIZE + 2 * RANK :, :] = jnp.zeros((PANEL - 2 * RANK, PANEL), F32)
    work[1, SIZE + 2 * RANK :, :] = jnp.zeros((PANEL - 2 * RANK, PANEL), F32)

    def step(k, carry):
        slot = lax.rem(k, 2)
        for copy in fetch(k, slot):
            copy.wait()

        @pl.when(k + 1 < COUNT)
        def _():
            for copy in fetch(k + 1, 1 - slot):
                copy.start()

        def rows_of(i):
            return pl.ds(pl.multiple_of(i * PANEL, PANEL), PANEL)

        def update(i, carry):
            def add(m, acc):
                left_high = high[m, rows_of(i), :]
                left_low = low[m, rows_of(i), :]
                right_high = high[m, rows_of(k), :]
                right_low = low[m, rows_of(k), :]
                dot = lambda a, b: lax.dot_general(a, b, NT, preferred_element_type=F32)
                return acc - (dot(left_high, right_high) + dot(left_high, right_low) + dot(left_low, right_high))

            work[slot, rows_of(i), :] = lax.fori_loop(0, k, add, work[slot, rows_of(i), :])
            return carry

        @pl.when(k > 0)
        def _():
            lax.fori_loop(k, COUNT + 1, update, 0)

        tile = work.at[slot, rows_of(k)]
        first_up, first_inv = factor_values(tile[:HALF, :HALF])
        cross = exact(tile[HALF:, :HALF], first_inv, NT)
        rest = tile[HALF:, HALF:] - exact(cross, cross, NT)
        second_up, second_inv = factor_values(rest)
        corner = -exact(second_inv, exact(cross, first_inv, NN), NN)
        zero = jnp.zeros((HALF, HALF), F32)
        inverse[:HALF, :HALF] = first_inv
        inverse[:HALF, HALF:] = zero
        inverse[HALF:, :HALF] = corner
        inverse[HALF:, HALF:] = second_inv
        tile[:HALF, :HALF] = first_up.T
        tile[:HALF, HALF:] = zero
        tile[HALF:, :HALF] = cross
        tile[HALF:, HALF:] = second_up.T

        def solve(i, carry):
            value = exact(work[slot, rows_of(i), :], inverse[...], NT)
            work[slot, rows_of(i), :] = value
            top, bottom = split(value)
            high[k, rows_of(i), :] = top
            low[k, rows_of(i), :] = bottom
            return carry

        lax.fori_loop(k + 1, COUNT + 1, solve, 0)
        cols = pl.ds(pl.multiple_of(k * PANEL, PANEL), PANEL)
        start = pl.multiple_of(own_tile * PANEL + own_row, 8)
        mine = work[slot, pl.ds(start, 8), :]
        own_ref[:, cols] = jnp.where(own_tile >= k, mine, 0.0)
        solved_ref[:, cols] = work[slot, SIZE : SIZE + 2 * RANK, :]
        return carry

    lax.fori_loop(0, COUNT, step, 0)
    coupling = exact(solved_ref[:RANK, :], solved_ref[RANK:, :], NT)
    grown_ref[:RANK, :] = trail_ref[...]
    grown_ref[RANK:, :] = -exact(coupling, base_ref[...], TN)


def panel_step(place, diag, pan, base, trail):
    vmem = pl.BlockSpec(memory_space=pltpu.VMEM)
    anywhere = pl.BlockSpec(memory_space=pl.ANY)
    return pl.pallas_call(
        panel_kernel,
        out_shape=(
            jax.ShapeDtypeStruct((8, SIZE), F32),
            jax.ShapeDtypeStruct((2 * RANK, SIZE), F32),
            jax.ShapeDtypeStruct((2 * RANK, SIZE), F32),
        ),
        in_specs=[pl.BlockSpec(memory_space=pltpu.SMEM), anywhere, anywhere, vmem, vmem],
        out_specs=(vmem, vmem, vmem),
        scratch_shapes=[
            pltpu.VMEM((2, SIZE + PANEL, PANEL), F32),
            pltpu.VMEM((COUNT, SIZE + PANEL, PANEL), BF16),
            pltpu.VMEM((COUNT, SIZE + PANEL, PANEL), BF16),
            pltpu.VMEM((PANEL, PANEL), F32),
            pltpu.SemaphoreType.DMA((2, 2)),
        ],
        compiler_params=pltpu.CompilerParams(vmem_limit_bytes=56 * 1024 * 1024),
    )(place, diag, pan, base, trail)


def body(diag_tile, row_pan_u, row_pan_v, col_pan_u, col_pan_v, trail_u, trail_v):
    row = lax.axis_index("row")
    col = lax.axis_index("col")
    diag = lax.all_gather(diag_tile, ("row", "col"), axis=0, tiled=True)
    row_all = lax.all_gather(jnp.stack([row_pan_u[0], row_pan_v[0]]), "col", axis=1, tiled=True)
    col_all = lax.all_gather(jnp.stack([col_pan_u[0], col_pan_v[0]]), "row", axis=1, tiled=True)
    pan = jnp.concatenate([row_all[1], col_all[1]], axis=0)
    place = jnp.stack([row, col * 8]).astype(jnp.int32)
    own, solved, grown_u = panel_step(place, diag, pan, row_all[0], trail_u[0, 0])
    row_own = lax.dynamic_slice_in_dim(solved, col * 2, 2, 0)
    col_own = lax.dynamic_slice_in_dim(solved, RANK + row * 8, 8, 0)
    grown_v = jnp.concatenate([trail_v[0, 0], col_all[0]], axis=0)
    return (own, row_own[None], col_own[None], grown_u[None, None], grown_v[None, None])


def solution(mesh):
    placed = (
        P(("row", "col"), None),
        P("row", "col", None),
        P("row", "col", None),
        P("col", "row", None),
        P("col", "row", None),
        P("row", "col", None, None),
        P("row", "col", None, None),
    )
    return jax.shard_map(
        body,
        mesh=mesh,
        in_specs=placed,
        out_specs=(
            P(("row", "col"), None),
            P("row", "col", None),
            P("col", "row", None),
            P("row", "col", None, None),
            P("row", "col", None, None),
        ),
        check_vma=False,
    )
```

```python
import jax
import jax.numpy as jnp
import numpy as np
from jax import lax
from jax.experimental import pallas as pl
from jax.experimental.pallas import tpu as pltpu
from jax.sharding import PartitionSpec as P

F32 = jnp.float32
BF16 = jnp.bfloat16
SIZE = 2048
PANEL = 256
COUNT = SIZE // PANEL
HALF = PANEL // 2
RANK = 64
NT = (((1,), (1,)), ((), ()))
TN = (((0,), (0,)), ((), ()))
NN = (((1,), (0,)), ((), ()))
EARLY = 2
LANES = COUNT * 4


def tile_start(k, first):
    return sum(COUNT - j for j in range(first, k))


def exact(left, right, dims):
    return lax.dot_general(left, right, dims, precision=lax.Precision.HIGHEST, preferred_element_type=F32)


def split(value):
    high = value.astype(BF16)
    return high, (value - high.astype(F32)).astype(BF16)


def iota(shape, dim):
    return lax.broadcasted_iota(jnp.int32, shape, dim)


def along_rows(value, row):
    return jnp.broadcast_to(value[row : row + 1, :], value.shape)


def along_lanes(value, lane):
    return jnp.broadcast_to(value[:, lane : lane + 1], value.shape)


def total(terms):
    while len(terms) > 1:
        terms = [
            terms[i] + terms[i + 1] if i + 1 < len(terms) else terms[i]
            for i in range(0, len(terms), 2)
        ]
    return terms[0]


def factor_block(block, beside, groups=2):
    count = len(block)
    size = 8 * count
    width = 8 * groups
    work = list(block)
    sub = iota((8, size), 0)
    lane = iota((8, size), 1)
    side = [jnp.where(sub + 8 * i == lane, 1.0, 0.0).astype(F32) for i in range(count)]
    upper = [None] * count
    inverse = [None] * count
    for top in range(0, count, groups):
        beside(top // groups)
        rows = work[top : top + groups]
        eyes = side[top : top + groups]
        cols = [[along_lanes(rows[a], 8 * top + k) for a in range(groups)] for k in range(width)]
        below = {
            i: [along_lanes(work[i], 8 * top + k) for k in range(width)]
            for i in range(top + groups, count)
        }
        up = [jnp.zeros((8, size), F32)] * groups
        inv = [jnp.zeros((8, size), F32)] * groups
        for k in range(width):
            ka, ks = divmod(k, 8)
            pivot = along_rows(cols[k][ka], ks)
            scale = 1.0 / pivot
            root = lax.rsqrt(pivot)
            row_k = along_rows(rows[ka], ks)
            eye_k = along_rows(eyes[ka], ks)
            here = sub == ks
            up[ka] = jnp.where(here, row_k * root, up[ka])
            inv[ka] = jnp.where(here, eye_k * root, inv[ka])
            times = []
            for a in range(groups):
                ratio = cols[k][a] * scale
                times.append(jnp.where(here, 1.0 - scale, ratio) if a == ka else ratio)
            for a in range(groups):
                rows[a] = rows[a] - times[a] * row_k
                eyes[a] = eyes[a] - times[a] * eye_k
            for m in range(k + 1, width):
                col_m = along_rows(cols[m][ka], ks)
                cols[m] = [cols[m][a] - times[a] * col_m for a in range(groups)]
        upper[top : top + groups] = up
        inverse[top : top + groups] = inv
        row_all = [along_rows(rows[k // 8], k % 8) for k in range(width)]
        eye_all = [along_rows(eyes[k // 8], k % 8) for k in range(width)]
        for i in range(top + groups, count):
            work[i] = work[i] - total([below[i][k] * row_all[k] for k in range(width)])
            side[i] = side[i] - total([below[i][k] * eye_all[k] for k in range(width)])
    upper = [jnp.where(sub + 8 * i <= lane, upper[i], 0.0) for i in range(count)]
    inverse = [jnp.where(sub + 8 * i >= lane, inverse[i], 0.0) for i in range(count)]
    return jnp.concatenate(upper, axis=0), jnp.concatenate(inverse, axis=0)


def factor_values(value, beside):
    return factor_block([value[8 * i : 8 * i + 8, :] for i in range(value.shape[0] // 8)], beside)


def dot3(left_high, left_low, right_high, right_low):
    left = jnp.concatenate([left_high, left_low, left_high], axis=1)
    right = jnp.concatenate([right_high, right_high, right_low], axis=1)
    return lax.dot_general(left, right, NT, preferred_element_type=F32)


def start_fetch(place_ref, mine_ref, other_ref, work, sems, first, last):
    x0, y0, core = place_ref[2], place_ref[3], place_ref[4]
    for k in range(first, last):
        at = tile_start(k, first)
        for source, owner in ((mine_ref, core), (other_ref, 1 - core)):
            for outer in range(4):
                for inner in range(4):
                    dx = jnp.where(owner == 0, outer, inner)
                    dy = jnp.where(owner == 0, inner, outer)
                    group = (lax.rem(x0 - dx + 4, 4) * 4 + lax.rem(y0 - dy + 4, 4)) * 2 + owner
                    pltpu.make_async_copy(
                        source.at[outer, inner, pl.ds(at, COUNT - k)],
                        work.at[k - first, pl.ds(k, COUNT - k), group],
                        sems.at[k - first],
                    ).start()


def wait_fetch(k, work, sems, first, last):
    for j in range(first, last):

        @pl.when(k == j)
        def _():
            whole = work.at[j - first, pl.ds(j, COUNT - j)]
            pltpu.make_async_copy(whole, whole, sems.at[j - first]).wait()


SOLVES = 6
UPDATES = 26


def plan(first, last, rows):
    spare = last - first
    table = []
    for k in range(first, last):
        solves, updates = [], []
        if k > first:
            solves = [(k - 1 - first, i, k - 1) for i in range(k + 1, rows)]
        for m in range(k if k == first else k - 1, -1, -1) if k == first else [k - 1]:
            if m < k:
                updates += [(k - first, k, i, m) for i in range(k + 1, rows)]
        if k + 1 < last:
            updates += [(k + 1 - first, k + 1, i, m) for i in range(k + 1, rows) for m in range(k)]
        assert len(solves) <= SOLVES and len(updates) <= UPDATES
        solves += [(spare, 0, COUNT)] * (SOLVES - len(solves))
        updates += [(spare, k, k, 0)] * (UPDATES - len(updates))
        table.append([x for t in solves + updates for x in t])
    return np.array(table, np.int32)


def factor_panel(tile, store, inverse, beside):
    first_up, first_inv = factor_values(tile[:HALF, :HALF], beside)
    cross = exact(tile[HALF:, :HALF], first_inv, NT)
    rest = tile[HALF:, HALF:] - exact(cross, cross, NT)
    steps = HALF // 16
    second_up, second_inv = factor_values(rest, lambda j: beside(j + steps))
    corner = -exact(second_inv, exact(cross, first_inv, NN), NN)
    zero = jnp.zeros((HALF, HALF), F32)
    inverse[:HALF, :HALF] = first_inv
    inverse[:HALF, HALF:] = zero
    inverse[HALF:, :HALF] = corner
    inverse[HALF:, HALF:] = second_inv
    top = jnp.concatenate([first_up.T, zero], axis=1)
    bottom = jnp.concatenate([cross, second_up.T], axis=1)
    store(jnp.concatenate([top, bottom], axis=0))


def factor_range(plan_ref, work, high, low, inverses, wait, first, last):
    def solve(slot, i, k, to):
        value = exact(work[slot, i].reshape(PANEL, PANEL), inverses[k], NT)
        work[slot, i] = value.reshape(LANES, 8, PANEL)
        top, bottom = split(value)
        high[to, i] = top
        low[to, i] = bottom

    def update(slot, k, i, m):
        value = dot3(high[m, i], low[m, i], high[m, k], low[m, k]).reshape(LANES, 8, PANEL)
        work[slot, i] = work[slot, i] - value

    wait(jnp.int32(first))
    for m in range(first):
        update(0, first, first, m)

    def step(k, carry):
        at = k - first
        wait(k + 1)

        @pl.when(k > first)
        def _():
            solve(at - 1, k, k - 1, k - 1)
            update(at, k, k, k - 1)

        def item(j):
            if j < SOLVES:
                slot, i, to = (plan_ref[at, 3 * j + x] for x in range(3))
                solve(slot, i, jnp.maximum(k - 1, first), to)
            elif j < SOLVES + UPDATES:
                base = 3 * SOLVES + 4 * (j - SOLVES)
                update(*(plan_ref[at, base + x] for x in range(4)))

        def beside(step):
            item(2 * step)
            item(2 * step + 1)

        def store(value):
            work[at, k] = value.reshape(LANES, 8, PANEL)

        factor_panel(work[at, k].reshape(PANEL, PANEL), store, inverses.at[k], beside)
        return carry

    lax.fori_loop(first, last, step, 0)
    return solve


def own_rows(place_ref, own_ref, work, first, last):
    own_tile, own_group = place_ref[0], place_ref[1]
    for k in range(first, last):
        mine = work[k - first, own_tile, own_group]
        own_ref[:, k * PANEL : (k + 1) * PANEL] = jnp.where(own_tile >= k, mine, 0.0)


def early_kernel(place_ref, plan_ref, mine_ref, other_ref, own_ref, high_ref, low_ref, inverse_ref, work, high, low, sems):
    start_fetch(place_ref, mine_ref, other_ref, work, sems, 0, EARLY)
    wait = lambda k: wait_fetch(k, work, sems, 0, EARLY)
    solve = factor_range(plan_ref, work, high, low, inverse_ref, wait, 0, EARLY)
    last = EARLY - 1
    for i in range(EARLY, COUNT):
        solve(last, i, last, last)
    high_ref[...] = high[:EARLY]
    low_ref[...] = low[:EARLY]
    own_rows(place_ref, own_ref, work, 0, EARLY)


def late_kernel(
    place_ref, plan_ref, mine_ref, other_ref, high_ref, low_ref, inverse_ref, early_ref, cols_ref, trail_u_ref, trail_v_ref,
    own_ref, row_ref, col_ref, grown_u_ref, grown_v_ref,
    work, high, low, inverses, rows_all, pan, base, solved, change, sems, more_sems,
):
    x0, y0, core = place_ref[2], place_ref[3], place_ref[4]
    last = COUNT - 1
    loads = []
    for j in range(EARLY):
        loads.append(pltpu.make_async_copy(high_ref.at[j], high.at[j, pl.ds(0, COUNT)], more_sems.at[3 * j]))
        loads.append(pltpu.make_async_copy(low_ref.at[j], low.at[j, pl.ds(0, COUNT)], more_sems.at[3 * j + 1]))
        loads.append(pltpu.make_async_copy(inverse_ref.at[j], inverses.at[j], more_sems.at[3 * j + 2]))
    loads.append(pltpu.make_async_copy(cols_ref.at[1], pan.at[pl.ds(RANK, RANK)], more_sems.at[3 * EARLY]))
    for copy in loads:
        copy.start()
    tiles = tile_start(COUNT, EARLY)
    row_sem = more_sems.at[3 * EARLY + 1]
    for source, owner in ((mine_ref, core), (other_ref, 1 - core)):
        for outer in range(4):
            for inner in range(4):
                dx = jnp.where(owner == 0, outer, inner)
                dy = jnp.where(owner == 0, inner, outer)
                group = (lax.rem(x0 - dx + 4, 4) * 4 + lax.rem(y0 - dy + 4, 4)) * 2 + owner
                pltpu.make_async_copy(source.at[outer, inner, pl.ds(tiles, 4)], rows_all.at[:, group], row_sem).start()
    start_fetch(place_ref, mine_ref, other_ref, work, sems, EARLY, COUNT)
    passing = [
        pltpu.make_async_copy(trail_u_ref, grown_u_ref.at[pl.ds(0, RANK)], more_sems.at[3 * EARLY + 2]),
        pltpu.make_async_copy(trail_v_ref, grown_v_ref.at[pl.ds(0, RANK)], more_sems.at[3 * EARLY + 3]),
        pltpu.make_async_copy(cols_ref.at[0], grown_v_ref.at[pl.ds(RANK, RANK)], more_sems.at[3 * EARLY + 4]),
    ]
    for copy in passing:
        copy.start()
    for copy in loads:
        copy.wait()
    pltpu.make_async_copy(rows_all, rows_all, row_sem).wait()
    for k in range(COUNT):
        cols = slice(k * PANEL, (k + 1) * PANEL)
        for r in range(2):
            base[32 * r : 32 * r + 32, cols] = rows_all[r, :, k, :]
            pan[32 * r : 32 * r + 32, cols] = rows_all[2 + r, :, k, :]
    empty = jnp.zeros((LANES // 2, 8, PANEL), F32)
    nothing = jnp.zeros((HALF, PANEL), BF16)
    for k in range(COUNT):
        cols = slice(k * PANEL, (k + 1) * PANEL)
        value = pan[:, cols]
        if k < EARLY:
            for m in range(k):
                value = value - dot3(high[m, COUNT, :HALF], low[m, COUNT, :HALF], high[m, k], low[m, k])
            value = exact(value, inverses[k], NT)
            solved[:, cols] = value
            high[k, COUNT, :HALF], low[k, COUNT, :HALF] = split(value)
            high[k, COUNT, HALF:] = nothing
            low[k, COUNT, HALF:] = nothing
        else:
            work[k - EARLY, COUNT, : LANES // 2] = value.reshape(LANES // 2, 8, PANEL)
            work[k - EARLY, COUNT, LANES // 2 :] = empty
    wait = lambda k: wait_fetch(k, work, sems, EARLY, COUNT)
    solve = factor_range(plan_ref, work, high, low, inverses, wait, EARLY, COUNT)
    solve(last - EARLY, COUNT, last, last)
    for k in range(EARLY, COUNT):
        solved[:, k * PANEL : (k + 1) * PANEL] = work[k - EARLY, COUNT, : LANES // 2].reshape(HALF, PANEL)
    coupling = exact(solved[:RANK, :], solved[RANK:, :], NT)
    change[...] = -exact(coupling, base[...], TN)
    out = pltpu.make_async_copy(change, grown_u_ref.at[pl.ds(RANK, RANK)], more_sems.at[3 * EARLY + 5])
    out.start()
    own_ref[:, : EARLY * PANEL] = early_ref[...]
    own_rows(place_ref, own_ref, work, EARLY, COUNT)
    for r in range(2):
        row_ref[r : r + 1, :] = solved[pl.ds(32 * r + place_ref[1], 1), :]
    col_ref[...] = solved[pl.ds(pl.multiple_of(RANK + place_ref[0] * 8, 8), 8), :]
    for copy in passing:
        copy.wait()
    out.wait()


VMEM = pl.BlockSpec(memory_space=pltpu.VMEM)
SMEM = pl.BlockSpec(memory_space=pltpu.SMEM)
ANYWHERE = pl.BlockSpec(memory_space=pl.ANY)
ROOM = pltpu.CompilerParams(vmem_limit_bytes=60 * 1024 * 1024)


def early_step(place, mine, other):
    return pl.pallas_call(
        early_kernel,
        out_shape=(
            jax.ShapeDtypeStruct((8, EARLY * PANEL), F32),
            jax.ShapeDtypeStruct((EARLY, COUNT, PANEL, PANEL), BF16),
            jax.ShapeDtypeStruct((EARLY, COUNT, PANEL, PANEL), BF16),
            jax.ShapeDtypeStruct((EARLY, PANEL, PANEL), F32),
        ),
        in_specs=[SMEM, SMEM, ANYWHERE, ANYWHERE],
        out_specs=(VMEM, VMEM, VMEM, VMEM),
        scratch_shapes=[
            pltpu.VMEM((EARLY + 1, COUNT, LANES, 8, PANEL), F32),
            pltpu.VMEM((COUNT + 1, COUNT, PANEL, PANEL), BF16),
            pltpu.VMEM((COUNT + 1, COUNT, PANEL, PANEL), BF16),
            pltpu.SemaphoreType.DMA((EARLY,)),
        ],
        compiler_params=ROOM,
        cost_estimate=pl.CostEstimate(flops=30 * 10**9, bytes_accessed=80 * 10**6, transcendentals=0),
    )(place, jnp.asarray(plan(0, EARLY, COUNT)), mine, other)


def late_step(place, mine, other, high, low, inverse, early, cols, trail_u, trail_v):
    late = COUNT - EARLY
    return pl.pallas_call(
        late_kernel,
        out_shape=(
            jax.ShapeDtypeStruct((8, SIZE), F32),
            jax.ShapeDtypeStruct((2, SIZE), F32),
            jax.ShapeDtypeStruct((8, SIZE), F32),
            jax.ShapeDtypeStruct((2 * RANK, SIZE), F32),
            jax.ShapeDtypeStruct((2 * RANK, SIZE), F32),
        ),
        in_specs=[SMEM, SMEM] + [ANYWHERE] * 5 + [VMEM] + [ANYWHERE] * 3,
        out_specs=(VMEM, VMEM, VMEM, ANYWHERE, ANYWHERE),
        scratch_shapes=[
            pltpu.VMEM((late + 1, COUNT + 1, LANES, 8, PANEL), F32),
            pltpu.VMEM((COUNT + 1, COUNT + 1, PANEL, PANEL), BF16),
            pltpu.VMEM((COUNT + 1, COUNT + 1, PANEL, PANEL), BF16),
            pltpu.VMEM((COUNT, PANEL, PANEL), F32),
            pltpu.VMEM((4, 32, 8, PANEL), F32),
            pltpu.VMEM((2 * RANK, SIZE), F32),
            pltpu.VMEM((RANK, SIZE), F32),
            pltpu.VMEM((2 * RANK, SIZE), F32),
            pltpu.VMEM((RANK, SIZE), F32),
            pltpu.SemaphoreType.DMA((late,)),
            pltpu.SemaphoreType.DMA((3 * EARLY + 6,)),
        ],
        compiler_params=ROOM,
        cost_estimate=pl.CostEstimate(flops=80 * 10**9, bytes_accessed=300 * 10**6, transcendentals=0),
    )(place, jnp.asarray(plan(EARLY, COUNT, COUNT + 1)), mine, other, high, low, inverse, early, cols, trail_u, trail_v)


def column(x, y, core):
    return (x % 4 * 4 + y % 4) * 2 + core


def ring(shift, stage):
    pairs = []
    for x in range(4):
        for y in range(4):
            for core in range(2):
                along_y = stage == core
                target = column(x, y + shift, core) if along_y else column(x + shift, y, core)
                pairs.append((column(x, y, core), target))
    return pairs


def spread_parts(piece, stage):
    return [piece] + [lax.ppermute(piece, "col", ring(s, stage)) for s in (1, 2, 3)]


def spread(piece, stage):
    return jnp.stack(spread_parts(piece, stage))


def tiles_of(bands, first, last):
    return jnp.concatenate([bands[k, k:] for k in range(first, last)], axis=0)


def swap(piece):
    return lax.ppermute(piece, "col", [(i, i ^ 1) for i in range(32)])


def body(diag_tile, row_pan_u, row_pan_v, col_pan_u, col_pan_v, trail_u, trail_v):
    row = lax.axis_index("row")
    col = lax.axis_index("col")
    cols = lax.all_gather(jnp.stack([col_pan_u[0], col_pan_v[0]]), "row", axis=1, tiled=True)
    copies = jnp.broadcast_to(diag_tile[None], (COUNT, 8, SIZE))
    bands = lax.all_to_all(copies, "row", 0, 0)
    bands = bands.reshape(COUNT, 8, COUNT, PANEL).transpose(2, 0, 1, 3)
    rows = jnp.concatenate([row_pan_u[0], row_pan_v[0]], axis=0).reshape(4, COUNT, PANEL)
    early = tiles_of(bands, 0, EARLY)
    late = jnp.concatenate([tiles_of(bands, EARLY, COUNT), rows], axis=0)
    early = spread(early, 0)
    early, late = lax.optimization_barrier((early, late))
    early = spread(early, 1)
    late = spread(late, 0)
    early_other = swap(early)
    early, early_other, late = lax.optimization_barrier((early, early_other, late))
    late = spread_parts(late, 1)
    place = jnp.stack([row, col, col // 8, col // 2 % 4, col % 2]).astype(jnp.int32)
    own, high, low, inverse = early_step(place, early, early_other)
    late, cols, high = lax.optimization_barrier((late, cols, high))
    late = jnp.stack(late)
    late_other = swap(late)
    own, row_own, col_own, grown_u, grown_v = late_step(
        place, late, late_other, high, low, inverse, own, cols, trail_u[0, 0], trail_v[0, 0]
    )
    return (own, row_own[None], col_own[None], grown_u[None, None], grown_v[None, None])


def solution(mesh):
    placed = (
        P(("row", "col"), None),
        P("row", "col", None),
        P("row", "col", None),
        P("col", "row", None),
        P("col", "row", None),
        P("row", "col", None, None),
        P("row", "col", None, None),
    )
    return jax.shard_map(
        body,
        mesh=mesh,
        in_specs=placed,
        out_specs=(
            P(("row", "col"), None),
            P("row", "col", None),
            P("col", "row", None),
            P("row", "col", None, None),
            P("row", "col", None, None),
        ),
        check_vma=False,
    )
```

```python
import functools

import jax
import jax.numpy as jnp
import numpy as np
from jax import lax
from jax.experimental import pallas as pl
from jax.experimental.pallas import tpu as pltpu
from jax.sharding import PartitionSpec as P

F32 = jnp.float32
BF16 = jnp.bfloat16
SIZE = 2048
PANEL = 256
COUNT = SIZE // PANEL
HALF = PANEL // 2
RANK = 64
NT = (((1,), (1,)), ((), ()))
TN = (((0,), (0,)), ((), ()))
NN = (((1,), (0,)), ((), ()))
EARLY = 2
LANES = COUNT * 4


def tile_start(k, first):
    return sum(COUNT - j for j in range(first, k))


def exact(left, right, dims):
    return lax.dot_general(left, right, dims, precision=lax.Precision.HIGHEST, preferred_element_type=F32)


def split(value):
    high = value.astype(BF16)
    return high, (value - high.astype(F32)).astype(BF16)


def iota(shape, dim):
    return lax.broadcasted_iota(jnp.int32, shape, dim)


def along_rows(value, row):
    return jnp.broadcast_to(value[row : row + 1, :], value.shape)


def along_lanes(value, lane):
    return jnp.broadcast_to(value[:, lane : lane + 1], value.shape)


def total(terms):
    while len(terms) > 1:
        terms = [
            terms[i] + terms[i + 1] if i + 1 < len(terms) else terms[i]
            for i in range(0, len(terms), 2)
        ]
    return terms[0]


def factor_block(block, beside, groups=2):
    count = len(block)
    size = 8 * count
    width = 8 * groups
    work = list(block)
    sub = iota((8, size), 0)
    lane = iota((8, size), 1)
    side = [jnp.where(sub + 8 * i == lane, 1.0, 0.0).astype(F32) for i in range(count)]
    upper = [None] * count
    inverse = [None] * count
    for top in range(0, count, groups):
        beside(top // groups)
        rows = work[top : top + groups]
        eyes = side[top : top + groups]
        near = range(top + groups, min(count, top + 2 * groups))
        cols = [[along_lanes(rows[a], 8 * top + k) for a in range(groups)] for k in range(width)]
        below = {i: [along_lanes(work[i], 8 * top + k) for k in range(width)] for i in near}
        raw = jnp.concatenate(rows, axis=0)
        up = [jnp.zeros((8, size), F32)] * groups
        inv = [jnp.zeros((8, size), F32)] * groups
        pivot = along_rows(cols[0][0], 0)
        for k in range(width):
            ka, ks = divmod(k, 8)
            scale = 1.0 / pivot
            root = lax.rsqrt(pivot)
            here = sub == ks
            heads = {m: along_rows(cols[m][ka], ks) for m in range(k + 1, width)}
            if k + 1 < width:
                na, ns = divmod(k + 1, 8)
                pivot = along_rows(cols[k + 1][na] - (cols[k][na] * heads[k + 1]) * scale, ns)
            row_k = along_rows(rows[ka], ks)
            eye_k = along_rows(eyes[ka], ks)
            up[ka] = jnp.where(here, row_k * root, up[ka])
            inv[ka] = jnp.where(here, eye_k * root, inv[ka])
            times = []
            for a in range(groups):
                ratio = cols[k][a] * scale
                times.append(jnp.where(here, 1.0 - scale, ratio) if a == ka else ratio)
            for a in range(groups):
                rows[a] = rows[a] - times[a] * row_k
                eyes[a] = eyes[a] - times[a] * eye_k
            for m in range(k + 1, width):
                cols[m] = [cols[m][a] - times[a] * heads[m] for a in range(groups)]
        upper[top : top + groups] = up
        inverse[top : top + groups] = inv
        row_all = [along_rows(rows[k // 8], k % 8) for k in range(width)]
        eye_all = [along_rows(eyes[k // 8], k % 8) for k in range(width)]
        for i in near:
            work[i] = work[i] - total([below[i][k] * row_all[k] for k in range(width)])
            side[i] = side[i] - total([below[i][k] * eye_all[k] for k in range(width)])
        if top + 2 * groups < count:
            both = [jnp.concatenate(rows, axis=0), jnp.concatenate(eyes, axis=0)]
            raw_high, raw_low = split(raw)
            high, low = split(jnp.concatenate(both, axis=1))
            change = lax.dot_general(
                jnp.concatenate([raw_high, raw_low, raw_high], axis=0),
                jnp.concatenate([high, high, low], axis=0),
                TN,
                preferred_element_type=F32,
            )
            for i in range(top + 2 * groups, count):
                work[i] = work[i] - change[8 * i : 8 * i + 8, :size]
                side[i] = side[i] - change[8 * i : 8 * i + 8, size:]
    upper = [jnp.where(sub + 8 * i <= lane, upper[i], 0.0) for i in range(count)]
    inverse = [jnp.where(sub + 8 * i >= lane, inverse[i], 0.0) for i in range(count)]
    return jnp.concatenate(upper, axis=0), jnp.concatenate(inverse, axis=0)


def factor_values(value, beside):
    return factor_block([value[8 * i : 8 * i + 8, :] for i in range(value.shape[0] // 8)], beside)


def dot3(left_high, left_low, right_high, right_low):
    left = jnp.concatenate([left_high, left_low, left_high], axis=1)
    right = jnp.concatenate([right_high, right_high, right_low], axis=1)
    return lax.dot_general(left, right, NT, preferred_element_type=F32)


def start_fetch(place_ref, mine_ref, other_ref, work, sems, first, last):
    x0, y0, core = place_ref[2], place_ref[3], place_ref[4]
    for k in range(first, last):
        at = tile_start(k, first)
        for source, owner in ((mine_ref, core), (other_ref, 1 - core)):
            for outer in range(4):
                for inner in range(4):
                    dx = jnp.where(owner == 0, outer, inner)
                    dy = jnp.where(owner == 0, inner, outer)
                    group = (lax.rem(x0 - dx + 4, 4) * 4 + lax.rem(y0 - dy + 4, 4)) * 2 + owner
                    pltpu.make_async_copy(
                        source.at[outer, inner, pl.ds(at, COUNT - k)],
                        work.at[k - first, pl.ds(k, COUNT - k), group],
                        sems.at[k - first],
                    ).start()


def wait_fetch(k, work, sems, first, last):
    for j in range(first, last):

        @pl.when(k == j)
        def _():
            whole = work.at[j - first, pl.ds(j, COUNT - j)]
            pltpu.make_async_copy(whole, whole, sems.at[j - first]).wait()


SOLVES = 5
UPDATES = 18
STEPS = 2 * (HALF // 16)


def plan(first, last, rows):
    spare = last - first
    left = {(p, i, m) for p in range(first, last) for i in range(p, rows) for m in range(p)}
    left -= {(first, first, m) for m in range(first)} | {(p, p, p - 1) for p in range(first, last)}
    table = []
    for k in range(first, last):
        solves = [(k - 1 - first, i, k - 1) for i in range(k + 1, rows)] if k > first else []
        ready = [t for t in left if t[2] < k and t[0] <= k + 1]
        due = lambda t: (t[0] - (t[0] == t[1]), t)
        taken = sorted(ready, key=due)[:UPDATES]
        left -= set(taken)
        assert len(solves) <= SOLVES and all(due(t)[0] > k for t in left)
        updates = [(p - first, p, i, m) for p, i, m in taken]
        solves += [(spare, 0, COUNT)] * (SOLVES - len(solves))
        updates += [(spare, k, k, 0)] * (UPDATES - len(updates))
        table.append([x for t in solves + updates for x in t])
    assert not left
    return np.array(table, np.int32)


def factor_panel(tile, store, inverse, beside):
    first_up, first_inv = factor_values(tile[:HALF, :HALF], beside)
    cross = exact(tile[HALF:, :HALF], first_inv, NT)
    rest = tile[HALF:, HALF:] - exact(cross, cross, NT)
    steps = HALF // 16
    second_up, second_inv = factor_values(rest, lambda j: beside(j + steps))
    corner = -exact(second_inv, exact(cross, first_inv, NN), NN)
    zero = jnp.zeros((HALF, HALF), F32)
    inverse[:HALF, :HALF] = first_inv
    inverse[:HALF, HALF:] = zero
    inverse[HALF:, :HALF] = corner
    inverse[HALF:, HALF:] = second_inv
    top = jnp.concatenate([first_up.T, zero], axis=1)
    bottom = jnp.concatenate([cross, second_up.T], axis=1)
    store(jnp.concatenate([top, bottom], axis=0))


def factor_range(plan_ref, work, high, low, inverses, wait, first, last):
    def solve(slot, i, k, to):
        value = exact(work[slot, i].reshape(PANEL, PANEL), inverses[k], NT)
        work[slot, i] = value.reshape(LANES, 8, PANEL)
        top, bottom = split(value)
        high[to, i] = top
        low[to, i] = bottom

    def update(slot, k, i, m):
        value = dot3(high[m, i], low[m, i], high[m, k], low[m, k]).reshape(LANES, 8, PANEL)
        work[slot, i] = work[slot, i] - value

    def step(k, at, items):
        def beside(j):
            share = lambda x: -(-x * len(items) // STEPS)
            for item in items[share(j) : share(j + 1)]:
                item()

        def store(value):
            work[at, k] = value.reshape(LANES, 8, PANEL)

        factor_panel(work[at, k].reshape(PANEL, PANEL), store, inverses.at[k], beside)

    def head(k, at):
        solve(at - 1, k, k - 1, k - 1)
        update(at, k, k, k - 1)

    def early():
        for k in range(first, last):
            wait(jnp.int32(k))
            items = []
            if k > first:
                head(k, k)
                items = [functools.partial(solve, k - 1, i, k - 1, k - 1) for i in range(k + 1, COUNT)]
                items += [functools.partial(update, k, k, i, k - 1) for i in range(k + 1, COUNT)]
            step(k, k, items)

    def late_step_of(k, carry):
        at = k - first
        wait(k + 1)

        @pl.when(k > first)
        def _():
            head(k, at)

        def item(j):
            if j < SOLVES:
                slot, i, to = (plan_ref[at, 3 * j + x] for x in range(3))
                solve(slot, i, jnp.maximum(k - 1, first), to)
            else:
                base = 3 * SOLVES + 4 * (j - SOLVES)
                update(*(plan_ref[at, base + x] for x in range(4)))

        step(k, at, [functools.partial(item, j) for j in range(SOLVES + UPDATES)])
        return carry

    if plan_ref is None:
        early()
    else:
        wait(jnp.int32(first))
        for m in range(first):
            update(0, first, first, m)
        lax.fori_loop(first, last, late_step_of, 0)
    return solve


def own_rows(place_ref, own_ref, work, first, last):
    own_tile, own_group = place_ref[0], place_ref[1]
    for k in range(first, last):
        mine = work[k - first, own_tile, own_group]
        own_ref[:, k * PANEL : (k + 1) * PANEL] = jnp.where(own_tile >= k, mine, 0.0)


def early_kernel(place_ref, mine_ref, other_ref, own_ref, high, low, inverse_ref, work, sems):
    start_fetch(place_ref, mine_ref, other_ref, work, sems, 0, EARLY)
    wait = lambda k: wait_fetch(k, work, sems, 0, EARLY)
    solve = factor_range(None, work, high, low, inverse_ref, wait, 0, EARLY)
    last = EARLY - 1
    for i in range(EARLY, COUNT):
        solve(last, i, last, last)
    own_rows(place_ref, own_ref, work, 0, EARLY)


def late_kernel(
    place_ref, plan_ref, mine_ref, other_ref, high_ref, low_ref, inverse_ref, early_ref, cols_ref, trail_u_ref, trail_v_ref,
    own_ref, row_ref, col_ref, grown_u_ref, grown_v_ref,
    work, high, low, inverses, rows_all, pan, base, solved, change, sems, more_sems,
):
    x0, y0, core = place_ref[2], place_ref[3], place_ref[4]
    last = COUNT - 1
    loads = []
    for j in range(EARLY):
        loads.append(pltpu.make_async_copy(high_ref.at[j], high.at[j, pl.ds(0, COUNT)], more_sems.at[3 * j]))
        loads.append(pltpu.make_async_copy(low_ref.at[j], low.at[j, pl.ds(0, COUNT)], more_sems.at[3 * j + 1]))
        loads.append(pltpu.make_async_copy(inverse_ref.at[j], inverses.at[j], more_sems.at[3 * j + 2]))
    loads.append(pltpu.make_async_copy(cols_ref.at[1], pan.at[pl.ds(RANK, RANK)], more_sems.at[3 * EARLY]))
    for copy in loads:
        copy.start()
    tiles = tile_start(COUNT, EARLY)
    row_sem = more_sems.at[3 * EARLY + 1]
    for source, owner in ((mine_ref, core), (other_ref, 1 - core)):
        for outer in range(4):
            for inner in range(4):
                dx = jnp.where(owner == 0, outer, inner)
                dy = jnp.where(owner == 0, inner, outer)
                group = (lax.rem(x0 - dx + 4, 4) * 4 + lax.rem(y0 - dy + 4, 4)) * 2 + owner
                pltpu.make_async_copy(source.at[outer, inner, pl.ds(tiles, 4)], rows_all.at[:, group], row_sem).start()
    start_fetch(place_ref, mine_ref, other_ref, work, sems, EARLY, COUNT)
    passing = [
        pltpu.make_async_copy(trail_u_ref, grown_u_ref.at[pl.ds(0, RANK)], more_sems.at[3 * EARLY + 2]),
        pltpu.make_async_copy(trail_v_ref, grown_v_ref.at[pl.ds(0, RANK)], more_sems.at[3 * EARLY + 3]),
        pltpu.make_async_copy(cols_ref.at[0], grown_v_ref.at[pl.ds(RANK, RANK)], more_sems.at[3 * EARLY + 4]),
    ]
    for copy in passing:
        copy.start()
    for copy in loads:
        copy.wait()
    pltpu.make_async_copy(rows_all, rows_all, row_sem).wait()
    for k in range(COUNT):
        cols = slice(k * PANEL, (k + 1) * PANEL)
        for r in range(2):
            base[32 * r : 32 * r + 32, cols] = rows_all[r, :, k, :]
            pan[32 * r : 32 * r + 32, cols] = rows_all[2 + r, :, k, :]
    empty = jnp.zeros((LANES // 2, 8, PANEL), F32)
    nothing = jnp.zeros((HALF, PANEL), BF16)
    for k in range(COUNT):
        cols = slice(k * PANEL, (k + 1) * PANEL)
        value = pan[:, cols]
        if k < EARLY:
            for m in range(k):
                value = value - dot3(high[m, COUNT, :HALF], low[m, COUNT, :HALF], high[m, k], low[m, k])
            value = exact(value, inverses[k], NT)
            solved[:, cols] = value
            high[k, COUNT, :HALF], low[k, COUNT, :HALF] = split(value)
            high[k, COUNT, HALF:] = nothing
            low[k, COUNT, HALF:] = nothing
        else:
            work[k - EARLY, COUNT, : LANES // 2] = value.reshape(LANES // 2, 8, PANEL)
            work[k - EARLY, COUNT, LANES // 2 :] = empty
    wait = lambda k: wait_fetch(k, work, sems, EARLY, COUNT)
    solve = factor_range(plan_ref, work, high, low, inverses, wait, EARLY, COUNT)
    solve(last - EARLY, COUNT, last, last)
    for k in range(EARLY, COUNT):
        solved[:, k * PANEL : (k + 1) * PANEL] = work[k - EARLY, COUNT, : LANES // 2].reshape(HALF, PANEL)
    coupling = exact(solved[:RANK, :], solved[RANK:, :], NT)
    change[...] = -exact(coupling, base[...], TN)
    out = pltpu.make_async_copy(change, grown_u_ref.at[pl.ds(RANK, RANK)], more_sems.at[3 * EARLY + 5])
    out.start()
    own_ref[:, : EARLY * PANEL] = early_ref[...]
    own_rows(place_ref, own_ref, work, EARLY, COUNT)
    for r in range(2):
        row_ref[r : r + 1, :] = solved[pl.ds(32 * r + place_ref[1], 1), :]
    col_ref[...] = solved[pl.ds(pl.multiple_of(RANK + place_ref[0] * 8, 8), 8), :]
    for copy in passing:
        copy.wait()
    out.wait()


VMEM = pl.BlockSpec(memory_space=pltpu.VMEM)
SMEM = pl.BlockSpec(memory_space=pltpu.SMEM)
ANYWHERE = pl.BlockSpec(memory_space=pl.ANY)
ROOM = pltpu.CompilerParams(vmem_limit_bytes=60 * 1024 * 1024)


def early_step(place, mine, other):
    return pl.pallas_call(
        early_kernel,
        out_shape=(
            jax.ShapeDtypeStruct((8, EARLY * PANEL), F32),
            jax.ShapeDtypeStruct((EARLY, COUNT, PANEL, PANEL), BF16),
            jax.ShapeDtypeStruct((EARLY, COUNT, PANEL, PANEL), BF16),
            jax.ShapeDtypeStruct((EARLY, PANEL, PANEL), F32),
        ),
        in_specs=[SMEM, ANYWHERE, ANYWHERE],
        out_specs=(VMEM, VMEM, VMEM, VMEM),
        scratch_shapes=[
            pltpu.VMEM((EARLY, COUNT, LANES, 8, PANEL), F32),
            pltpu.SemaphoreType.DMA((EARLY,)),
        ],
        compiler_params=ROOM,
        cost_estimate=pl.CostEstimate(flops=30 * 10**9, bytes_accessed=80 * 10**6, transcendentals=0),
    )(place, mine, other)


def late_step(place, mine, other, high, low, inverse, early, cols, trail_u, trail_v):
    late = COUNT - EARLY
    return pl.pallas_call(
        late_kernel,
        out_shape=(
            jax.ShapeDtypeStruct((8, SIZE), F32),
            jax.ShapeDtypeStruct((2, SIZE), F32),
            jax.ShapeDtypeStruct((8, SIZE), F32),
            jax.ShapeDtypeStruct((2 * RANK, SIZE), F32),
            jax.ShapeDtypeStruct((2 * RANK, SIZE), F32),
        ),
        in_specs=[SMEM, SMEM] + [ANYWHERE] * 5 + [VMEM] + [ANYWHERE] * 3,
        out_specs=(VMEM, VMEM, VMEM, ANYWHERE, ANYWHERE),
        scratch_shapes=[
            pltpu.VMEM((late + 1, COUNT + 1, LANES, 8, PANEL), F32),
            pltpu.VMEM((COUNT + 1, COUNT + 1, PANEL, PANEL), BF16),
            pltpu.VMEM((COUNT + 1, COUNT + 1, PANEL, PANEL), BF16),
            pltpu.VMEM((COUNT, PANEL, PANEL), F32),
            pltpu.VMEM((4, 32, 8, PANEL), F32),
            pltpu.VMEM((2 * RANK, SIZE), F32),
            pltpu.VMEM((RANK, SIZE), F32),
            pltpu.VMEM((2 * RANK, SIZE), F32),
            pltpu.VMEM((RANK, SIZE), F32),
            pltpu.SemaphoreType.DMA((late,)),
            pltpu.SemaphoreType.DMA((3 * EARLY + 6,)),
        ],
        compiler_params=ROOM,
        cost_estimate=pl.CostEstimate(flops=80 * 10**9, bytes_accessed=300 * 10**6, transcendentals=0),
    )(place, jnp.asarray(plan(EARLY, COUNT, COUNT + 1)), mine, other, high, low, inverse, early, cols, trail_u, trail_v)


def column(x, y, core):
    return (x % 4 * 4 + y % 4) * 2 + core


def ring(shift, stage):
    pairs = []
    for x in range(4):
        for y in range(4):
            for core in range(2):
                along_y = stage == core
                target = column(x, y + shift, core) if along_y else column(x + shift, y, core)
                pairs.append((column(x, y, core), target))
    return pairs


def spread_parts(piece, stage):
    return [piece] + [lax.ppermute(piece, "col", ring(s, stage)) for s in (1, 2, 3)]


def spread(piece, stage):
    return jnp.stack(spread_parts(piece, stage))


def tiles_of(bands, first, last):
    return jnp.concatenate([bands[k, k:] for k in range(first, last)], axis=0)


def swap(piece):
    return lax.ppermute(piece, "col", [(i, i ^ 1) for i in range(32)])


def body(diag_tile, row_pan_u, row_pan_v, col_pan_u, col_pan_v, trail_u, trail_v):
    row = lax.axis_index("row")
    col = lax.axis_index("col")
    cols = lax.all_gather(jnp.stack([col_pan_u[0], col_pan_v[0]]), "row", axis=1, tiled=True)
    copies = jnp.broadcast_to(diag_tile[None], (COUNT, 8, SIZE))
    bands = lax.all_to_all(copies, "row", 0, 0)
    bands = bands.reshape(COUNT, 8, COUNT, PANEL).transpose(2, 0, 1, 3)
    rows = jnp.concatenate([row_pan_u[0], row_pan_v[0]], axis=0).reshape(4, COUNT, PANEL)
    count = tile_start(EARLY, 0)
    tiles = jnp.concatenate([tiles_of(bands, 0, EARLY), tiles_of(bands, EARLY, COUNT), rows], axis=0)
    tiles = spread_parts(tiles, 0)
    early = spread(jnp.stack([part[:count] for part in tiles]), 1)
    early_other = swap(early)
    early, tiles = lax.optimization_barrier((early, tiles))
    late = spread_parts(jnp.stack([part[count:] for part in tiles]), 1)
    place = jnp.stack([row, col, col // 8, col // 2 % 4, col % 2]).astype(jnp.int32)
    own, high, low, inverse = early_step(place, early, early_other)
    late, cols, high = lax.optimization_barrier((late, cols, high))
    late = jnp.stack(late)
    late_other = swap(late)
    own, row_own, col_own, grown_u, grown_v = late_step(
        place, late, late_other, high, low, inverse, own, cols, trail_u[0, 0], trail_v[0, 0]
    )
    return (own, row_own[None], col_own[None], grown_u[None, None], grown_v[None, None])


def solution(mesh):
    placed = (
        P(("row", "col"), None),
        P("row", "col", None),
        P("row", "col", None),
        P("col", "row", None),
        P("col", "row", None),
        P("row", "col", None, None),
        P("row", "col", None, None),
    )
    return jax.shard_map(
        body,
        mesh=mesh,
        in_specs=placed,
        out_specs=(
            P(("row", "col"), None),
            P("row", "col", None),
            P("col", "row", None),
            P("row", "col", None, None),
            P("row", "col", None, None),
        ),
        check_vma=False,
    )
```

```python
import functools

import jax
import jax.numpy as jnp
import numpy as np
from jax import lax
from jax.experimental import pallas as pl
from jax.experimental.pallas import tpu as pltpu
from jax.sharding import PartitionSpec as P

F32 = jnp.float32
BF16 = jnp.bfloat16
SIZE = 2048
PANEL = 256
COUNT = SIZE // PANEL
HALF = PANEL // 2
RANK = 64
NT = (((1,), (1,)), ((), ()))
TN = (((0,), (0,)), ((), ()))
NN = (((1,), (0,)), ((), ()))
EARLY = 2
LANES = COUNT * 4


def tile_start(k, first):
    return sum(COUNT - j for j in range(first, k))


def exact(left, right, dims):
    return lax.dot_general(left, right, dims, precision=lax.Precision.HIGHEST, preferred_element_type=F32)


def split(value):
    high = value.astype(BF16)
    return high, (value - high.astype(F32)).astype(BF16)


def iota(shape, dim):
    return lax.broadcasted_iota(jnp.int32, shape, dim)


def along_rows(value, row):
    return jnp.broadcast_to(value[row : row + 1, :], value.shape)


def along_lanes(value, lane):
    return jnp.broadcast_to(value[:, lane : lane + 1], value.shape)


def total(terms):
    while len(terms) > 1:
        terms = [
            terms[i] + terms[i + 1] if i + 1 < len(terms) else terms[i]
            for i in range(0, len(terms), 2)
        ]
    return terms[0]


def factor_block(block, beside, groups=2):
    count = len(block)
    size = 8 * count
    width = 8 * groups
    work = list(block)
    sub = iota((8, size), 0)
    lane = iota((8, size), 1)
    side = [jnp.where(sub + 8 * i == lane, 1.0, 0.0).astype(F32) for i in range(count)]
    upper = [None] * count
    inverse = [None] * count
    for top in range(0, count, groups):
        beside(top // groups)
        rows = work[top : top + groups]
        eyes = side[top : top + groups]
        near = range(top + groups, min(count, top + 2 * groups))
        cols = [[along_lanes(rows[a], 8 * top + k) for a in range(groups)] for k in range(width)]
        below = {i: [along_lanes(work[i], 8 * top + k) for k in range(width)] for i in near}
        raw = jnp.concatenate(rows, axis=0)
        up = [jnp.zeros((8, size), F32)] * groups
        inv = [jnp.zeros((8, size), F32)] * groups
        pivot = along_rows(cols[0][0], 0)
        for k in range(width):
            ka, ks = divmod(k, 8)
            scale = 1.0 / pivot
            root = lax.rsqrt(pivot)
            here = sub == ks
            heads = {m: along_rows(cols[m][ka], ks) for m in range(k + 1, width)}
            if k + 1 < width:
                na, ns = divmod(k + 1, 8)
                pivot = along_rows(cols[k + 1][na] - (cols[k][na] * heads[k + 1]) * scale, ns)
            row_k = along_rows(rows[ka], ks)
            eye_k = along_rows(eyes[ka], ks)
            up[ka] = jnp.where(here, row_k * root, up[ka])
            inv[ka] = jnp.where(here, eye_k * root, inv[ka])
            times = []
            for a in range(groups):
                ratio = cols[k][a] * scale
                times.append(jnp.where(here, 1.0 - scale, ratio) if a == ka else ratio)
            for a in range(groups):
                rows[a] = rows[a] - times[a] * row_k
                eyes[a] = eyes[a] - times[a] * eye_k
            for m in range(k + 1, width):
                cols[m] = [cols[m][a] - times[a] * heads[m] for a in range(groups)]
        upper[top : top + groups] = up
        inverse[top : top + groups] = inv
        row_all = [along_rows(rows[k // 8], k % 8) for k in range(width)]
        eye_all = [along_rows(eyes[k // 8], k % 8) for k in range(width)]
        for i in near:
            work[i] = work[i] - total([below[i][k] * row_all[k] for k in range(width)])
            side[i] = side[i] - total([below[i][k] * eye_all[k] for k in range(width)])
        if top + 2 * groups < count:
            both = [jnp.concatenate(rows, axis=0), jnp.concatenate(eyes, axis=0)]
            raw_high, raw_low = split(raw)
            high, low = split(jnp.concatenate(both, axis=1))
            change = lax.dot_general(
                jnp.concatenate([raw_high, raw_low, raw_high], axis=0),
                jnp.concatenate([high, high, low], axis=0),
                TN,
                preferred_element_type=F32,
            )
            for i in range(top + 2 * groups, count):
                work[i] = work[i] - change[8 * i : 8 * i + 8, :size]
                side[i] = side[i] - change[8 * i : 8 * i + 8, size:]
    upper = [jnp.where(sub + 8 * i <= lane, upper[i], 0.0) for i in range(count)]
    inverse = [jnp.where(sub + 8 * i >= lane, inverse[i], 0.0) for i in range(count)]
    return jnp.concatenate(upper, axis=0), jnp.concatenate(inverse, axis=0)


def factor_values(value, beside):
    return factor_block([value[8 * i : 8 * i + 8, :] for i in range(value.shape[0] // 8)], beside)


def dot3(left_high, left_low, right_high, right_low):
    left = jnp.concatenate([left_high, left_low, left_high], axis=1)
    right = jnp.concatenate([right_high, right_high, right_low], axis=1)
    return lax.dot_general(left, right, NT, preferred_element_type=F32)


def start_fetch(place_ref, mine_ref, other_ref, work, sems, first, last):
    x0, y0, core = place_ref[2], place_ref[3], place_ref[4]
    for k in range(first, last):
        at = tile_start(k, first)
        for source, owner in ((mine_ref, core), (other_ref, 1 - core)):
            for outer in range(4):
                for inner in range(4):
                    dx = jnp.where(owner == 0, outer, inner)
                    dy = jnp.where(owner == 0, inner, outer)
                    group = (lax.rem(x0 - dx + 4, 4) * 4 + lax.rem(y0 - dy + 4, 4)) * 2 + owner
                    pltpu.make_async_copy(
                        source.at[outer, inner, pl.ds(at, COUNT - k)],
                        work.at[k - first, pl.ds(k, COUNT - k), group],
                        sems.at[k - first],
                    ).start()


def wait_fetch(k, work, sems, first, last):
    for j in range(first, last):

        @pl.when(k == j)
        def _():
            whole = work.at[j - first, pl.ds(j, COUNT - j)]
            pltpu.make_async_copy(whole, whole, sems.at[j - first]).wait()


SOLVES = 5
UPDATES = 18
STEPS = 2 * (HALF // 16)


def plan(first, last, rows):
    spare = last - first
    left = {(p, i, m) for p in range(first, last) for i in range(p, rows) for m in range(p)}
    left -= {(first, first, m) for m in range(first)} | {(p, p, p - 1) for p in range(first, last)}
    table = []
    for k in range(first, last):
        solves = [(k - 1 - first, i, k - 1) for i in range(k + 1, rows)] if k > first else []
        ready = [t for t in left if t[2] < k and t[0] <= k + 1]
        due = lambda t: (t[0] - (t[0] == t[1]), t)
        taken = sorted(ready, key=due)[:UPDATES]
        left -= set(taken)
        assert len(solves) <= SOLVES and all(due(t)[0] > k for t in left)
        updates = [(p - first, p, i, m) for p, i, m in taken]
        solves += [(spare, 0, COUNT)] * (SOLVES - len(solves))
        updates += [(spare, k, k, 0)] * (UPDATES - len(updates))
        table.append([x for t in solves + updates for x in t])
    assert not left
    return np.array(table, np.int32)


def factor_panel(tile, store, inverse, beside):
    first_up, first_inv = factor_values(tile[:HALF, :HALF], beside)
    cross = exact(tile[HALF:, :HALF], first_inv, NT)
    rest = tile[HALF:, HALF:] - exact(cross, cross, NT)
    steps = HALF // 16
    second_up, second_inv = factor_values(rest, lambda j: beside(j + steps))
    corner = -exact(second_inv, exact(cross, first_inv, NN), NN)
    zero = jnp.zeros((HALF, HALF), F32)
    inverse[:HALF, :HALF] = first_inv
    inverse[:HALF, HALF:] = zero
    inverse[HALF:, :HALF] = corner
    inverse[HALF:, HALF:] = second_inv
    top = jnp.concatenate([first_up.T, zero], axis=1)
    bottom = jnp.concatenate([cross, second_up.T], axis=1)
    store(jnp.concatenate([top, bottom], axis=0))


def factor_range(plan_ref, work, high, low, inverses, wait, first, last):
    def solve(slot, i, k, to):
        value = exact(work[slot, i].reshape(PANEL, PANEL), inverses[k], NT)
        work[slot, i] = value.reshape(LANES, 8, PANEL)
        top, bottom = split(value)
        high[to, i] = top
        low[to, i] = bottom

    def update(slot, k, i, m):
        value = dot3(high[m, i], low[m, i], high[m, k], low[m, k]).reshape(LANES, 8, PANEL)
        work[slot, i] = work[slot, i] - value

    def step(k, at, items):
        def beside(j):
            share = lambda x: -(-x * len(items) // STEPS)
            for item in items[share(j) : share(j + 1)]:
                item()

        def store(value):
            work[at, k] = value.reshape(LANES, 8, PANEL)

        factor_panel(work[at, k].reshape(PANEL, PANEL), store, inverses.at[k], beside)

    def head(k, at):
        solve(at - 1, k, k - 1, k - 1)
        update(at, k, k, k - 1)

    def early():
        for k in range(first, last):
            wait(jnp.int32(k))
            items = []
            if k > first:
                head(k, k)
                items = [functools.partial(solve, k - 1, i, k - 1, k - 1) for i in range(k + 1, COUNT)]
                items += [functools.partial(update, k, k, i, k - 1) for i in range(k + 1, COUNT)]
            step(k, k, items)

    def late_step_of(k, carry):
        at = k - first
        wait(k + 1)

        @pl.when(k > first)
        def _():
            head(k, at)

        def item(j):
            if j < SOLVES:
                slot, i, to = (plan_ref[at, 3 * j + x] for x in range(3))
                solve(slot, i, jnp.maximum(k - 1, first), to)
            else:
                base = 3 * SOLVES + 4 * (j - SOLVES)
                update(*(plan_ref[at, base + x] for x in range(4)))

        step(k, at, [functools.partial(item, j) for j in range(SOLVES + UPDATES)])
        return carry

    if plan_ref is None:
        early()
    else:
        wait(jnp.int32(first))
        for m in range(first):
            update(0, first, first, m)
        lax.fori_loop(first, last, late_step_of, 0)
    return solve


def own_rows(place_ref, own_ref, work, first, last):
    own_tile, own_group = place_ref[0], place_ref[1]
    for k in range(first, last):
        mine = work[k - first, own_tile, own_group]
        own_ref[:, k * PANEL : (k + 1) * PANEL] = jnp.where(own_tile >= k, mine, 0.0)


def early_kernel(place_ref, mine_ref, other_ref, own_ref, high, low, inverse_ref, work, sems):
    start_fetch(place_ref, mine_ref, other_ref, work, sems, 0, EARLY)
    wait = lambda k: wait_fetch(k, work, sems, 0, EARLY)
    solve = factor_range(None, work, high, low, inverse_ref, wait, 0, EARLY)
    last = EARLY - 1
    for i in range(EARLY, COUNT):
        solve(last, i, last, last)
    own_rows(place_ref, own_ref, work, 0, EARLY)


def late_kernel(
    place_ref, plan_ref, mine_ref, other_ref, high_ref, low_ref, inverse_ref, early_ref, cols_ref, cols_other_ref, trail_u_ref, trail_v_ref,
    own_ref, row_ref, col_ref, grown_u_ref, grown_v_ref,
    work, high, low, inverses, rows_all, pan, base, solved, change, sems, more_sems,
):
    x0, y0, core = place_ref[2], place_ref[3], place_ref[4]
    last = COUNT - 1
    loads = []
    for j in range(EARLY):
        loads.append(pltpu.make_async_copy(high_ref.at[j], high.at[j, pl.ds(0, COUNT)], more_sems.at[3 * j]))
        loads.append(pltpu.make_async_copy(low_ref.at[j], low.at[j, pl.ds(0, COUNT)], more_sems.at[3 * j + 1]))
        loads.append(pltpu.make_async_copy(inverse_ref.at[j], inverses.at[j], more_sems.at[3 * j + 2]))
    for copy in loads:
        copy.start()
    tiles = tile_start(COUNT, EARLY)
    row_sem = more_sems.at[3 * EARLY + 1]
    for source, owner in ((mine_ref, core), (other_ref, 1 - core)):
        for outer in range(4):
            for inner in range(4):
                dx = jnp.where(owner == 0, outer, inner)
                dy = jnp.where(owner == 0, inner, outer)
                group = (lax.rem(x0 - dx + 4, 4) * 4 + lax.rem(y0 - dy + 4, 4)) * 2 + owner
                pltpu.make_async_copy(source.at[outer, inner, pl.ds(tiles, 4)], rows_all.at[:, group], row_sem).start()
    start_fetch(place_ref, mine_ref, other_ref, work, sems, EARLY, COUNT)
    column_pieces = []
    for source, first_bit in ((cols_ref, 0), (cols_other_ref, 1)):
        for second in range(2):
            for third in range(2):
                place = (place_ref[0] ^ (4 * third + 2 * second + first_bit)) * 8
                column_pieces.append((source.at[second, third], pl.multiple_of(place, 8)))
    col_sem, out_sem = more_sems.at[3 * EARLY], more_sems.at[3 * EARLY + 4]
    for source, place in column_pieces:
        pltpu.make_async_copy(source.at[1], pan.at[pl.ds(RANK + place, 8)], col_sem).start()
        pltpu.make_async_copy(source.at[0], grown_v_ref.at[pl.ds(RANK + place, 8)], out_sem).start()
    passing = [
        pltpu.make_async_copy(trail_u_ref, grown_u_ref.at[pl.ds(0, RANK)], more_sems.at[3 * EARLY + 2]),
        pltpu.make_async_copy(trail_v_ref, grown_v_ref.at[pl.ds(0, RANK)], more_sems.at[3 * EARLY + 3]),
    ]
    for copy in passing:
        copy.start()
    for copy in loads:
        copy.wait()
    pltpu.make_async_copy(rows_all, rows_all, row_sem).wait()
    pltpu.make_async_copy(pan.at[pl.ds(RANK, RANK)], pan.at[pl.ds(RANK, RANK)], col_sem).wait()
    for k in range(COUNT):
        cols = slice(k * PANEL, (k + 1) * PANEL)
        for r in range(2):
            base[32 * r : 32 * r + 32, cols] = rows_all[r, :, k, :]
            pan[32 * r : 32 * r + 32, cols] = rows_all[2 + r, :, k, :]
    empty = jnp.zeros((LANES // 2, 8, PANEL), F32)
    nothing = jnp.zeros((HALF, PANEL), BF16)
    for k in range(COUNT):
        cols = slice(k * PANEL, (k + 1) * PANEL)
        value = pan[:, cols]
        if k < EARLY:
            for m in range(k):
                value = value - dot3(high[m, COUNT, :HALF], low[m, COUNT, :HALF], high[m, k], low[m, k])
            value = exact(value, inverses[k], NT)
            solved[:, cols] = value
            high[k, COUNT, :HALF], low[k, COUNT, :HALF] = split(value)
            high[k, COUNT, HALF:] = nothing
            low[k, COUNT, HALF:] = nothing
        else:
            work[k - EARLY, COUNT, : LANES // 2] = value.reshape(LANES // 2, 8, PANEL)
            work[k - EARLY, COUNT, LANES // 2 :] = empty
    wait = lambda k: wait_fetch(k, work, sems, EARLY, COUNT)
    solve = factor_range(plan_ref, work, high, low, inverses, wait, EARLY, COUNT)
    solve(last - EARLY, COUNT, last, last)
    for k in range(EARLY, COUNT):
        solved[:, k * PANEL : (k + 1) * PANEL] = work[k - EARLY, COUNT, : LANES // 2].reshape(HALF, PANEL)
    coupling = exact(solved[:RANK, :], solved[RANK:, :], NT)
    change[...] = -exact(coupling, base[...], TN)
    out = pltpu.make_async_copy(change, grown_u_ref.at[pl.ds(RANK, RANK)], more_sems.at[3 * EARLY + 5])
    out.start()
    own_ref[:, : EARLY * PANEL] = early_ref[...]
    own_rows(place_ref, own_ref, work, EARLY, COUNT)
    for r in range(2):
        row_ref[r : r + 1, :] = solved[pl.ds(32 * r + place_ref[1], 1), :]
    col_ref[...] = solved[pl.ds(pl.multiple_of(RANK + place_ref[0] * 8, 8), 8), :]
    for copy in passing:
        copy.wait()
    whole = grown_v_ref.at[pl.ds(RANK, RANK)]
    pltpu.make_async_copy(whole, whole, out_sem).wait()
    out.wait()


VMEM = pl.BlockSpec(memory_space=pltpu.VMEM)
SMEM = pl.BlockSpec(memory_space=pltpu.SMEM)
ANYWHERE = pl.BlockSpec(memory_space=pl.ANY)
ROOM = pltpu.CompilerParams(vmem_limit_bytes=60 * 1024 * 1024)


def early_step(place, mine, other):
    return pl.pallas_call(
        early_kernel,
        out_shape=(
            jax.ShapeDtypeStruct((8, EARLY * PANEL), F32),
            jax.ShapeDtypeStruct((EARLY, COUNT, PANEL, PANEL), BF16),
            jax.ShapeDtypeStruct((EARLY, COUNT, PANEL, PANEL), BF16),
            jax.ShapeDtypeStruct((EARLY, PANEL, PANEL), F32),
        ),
        in_specs=[SMEM, ANYWHERE, ANYWHERE],
        out_specs=(VMEM, VMEM, VMEM, VMEM),
        scratch_shapes=[
            pltpu.VMEM((EARLY, COUNT, LANES, 8, PANEL), F32),
            pltpu.SemaphoreType.DMA((EARLY,)),
        ],
        compiler_params=ROOM,
        cost_estimate=pl.CostEstimate(flops=30 * 10**9, bytes_accessed=80 * 10**6, transcendentals=0),
    )(place, mine, other)


def late_step(place, mine, other, high, low, inverse, early, cols, cols_other, trail_u, trail_v):
    late = COUNT - EARLY
    return pl.pallas_call(
        late_kernel,
        out_shape=(
            jax.ShapeDtypeStruct((8, SIZE), F32),
            jax.ShapeDtypeStruct((2, SIZE), F32),
            jax.ShapeDtypeStruct((8, SIZE), F32),
            jax.ShapeDtypeStruct((2 * RANK, SIZE), F32),
            jax.ShapeDtypeStruct((2 * RANK, SIZE), F32),
        ),
        in_specs=[SMEM, SMEM] + [ANYWHERE] * 5 + [VMEM] + [ANYWHERE] * 4,
        out_specs=(VMEM, VMEM, VMEM, ANYWHERE, ANYWHERE),
        scratch_shapes=[
            pltpu.VMEM((late + 1, COUNT + 1, LANES, 8, PANEL), F32),
            pltpu.VMEM((COUNT + 1, COUNT + 1, PANEL, PANEL), BF16),
            pltpu.VMEM((COUNT + 1, COUNT + 1, PANEL, PANEL), BF16),
            pltpu.VMEM((COUNT, PANEL, PANEL), F32),
            pltpu.VMEM((4, 32, 8, PANEL), F32),
            pltpu.VMEM((2 * RANK, SIZE), F32),
            pltpu.VMEM((RANK, SIZE), F32),
            pltpu.VMEM((2 * RANK, SIZE), F32),
            pltpu.VMEM((RANK, SIZE), F32),
            pltpu.SemaphoreType.DMA((late,)),
            pltpu.SemaphoreType.DMA((3 * EARLY + 6,)),
        ],
        compiler_params=ROOM,
        cost_estimate=pl.CostEstimate(flops=80 * 10**9, bytes_accessed=300 * 10**6, transcendentals=0),
    )(place, jnp.asarray(plan(EARLY, COUNT, COUNT + 1)), mine, other, high, low, inverse, early, cols, cols_other, trail_u, trail_v)


def column(x, y, core):
    return (x % 4 * 4 + y % 4) * 2 + core


def ring(shift, stage):
    pairs = []
    for x in range(4):
        for y in range(4):
            for core in range(2):
                along_y = stage == core
                target = column(x, y + shift, core) if along_y else column(x + shift, y, core)
                pairs.append((column(x, y, core), target))
    return pairs


def spread_parts(piece, stage):
    return [piece] + [lax.ppermute(piece, "col", ring(s, stage)) for s in (1, 2, 3)]


def spread(piece, stage):
    return jnp.stack(spread_parts(piece, stage))


def tiles_of(bands, first, last):
    return jnp.concatenate([bands[k, k:] for k in range(first, last)], axis=0)


def swap(piece):
    return lax.ppermute(piece, "col", [(i, i ^ 1) for i in range(32)])


def across(piece, bit):
    return lax.ppermute(piece, "row", [(i, i ^ bit) for i in range(8)])


def body(diag_tile, row_pan_u, row_pan_v, col_pan_u, col_pan_v, trail_u, trail_v):
    row = lax.axis_index("row")
    col = lax.axis_index("col")
    copies = jnp.broadcast_to(diag_tile[None], (COUNT, 8, SIZE))
    bands = lax.all_to_all(copies, "row", 0, 0)
    bands = bands.reshape(COUNT, 8, COUNT, PANEL).transpose(2, 0, 1, 3)
    rows = jnp.concatenate([row_pan_u[0], row_pan_v[0]], axis=0).reshape(4, COUNT, PANEL)
    count = tile_start(EARLY, 0)
    tiles = jnp.concatenate([tiles_of(bands, 0, EARLY), tiles_of(bands, EARLY, COUNT), rows], axis=0)
    cols = lax.optimization_barrier((jnp.stack([col_pan_u[0], col_pan_v[0]]), bands))[0]
    cols = jnp.stack([cols, across(cols, 4)])
    tiles = spread_parts(tiles, 0)
    tiles, cols = lax.optimization_barrier((tiles, cols))
    cols = jnp.stack([cols, across(cols, 2)])
    early = spread(jnp.stack([part[:count] for part in tiles]), 1)
    early, cols = lax.optimization_barrier((early, cols))
    early_other = swap(early)
    cols_other = across(cols, 1)
    early, tiles = lax.optimization_barrier((early, tiles))
    late = spread_parts(jnp.stack([part[count:] for part in tiles]), 1)
    place = jnp.stack([row, col, col // 8, col // 2 % 4, col % 2]).astype(jnp.int32)
    own, high, low, inverse = early_step(place, early, early_other)
    late, cols_other, high = lax.optimization_barrier((late, cols_other, high))
    late = jnp.stack(late)
    late_other = swap(late)
    own, row_own, col_own, grown_u, grown_v = late_step(
        place, late, late_other, high, low, inverse, own, cols, cols_other, trail_u[0, 0], trail_v[0, 0]
    )
    return (own, row_own[None], col_own[None], grown_u[None, None], grown_v[None, None])


def solution(mesh):
    placed = (
        P(("row", "col"), None),
        P("row", "col", None),
        P("row", "col", None),
        P("col", "row", None),
        P("col", "row", None),
        P("row", "col", None, None),
        P("row", "col", None, None),
    )
    return jax.shard_map(
        body,
        mesh=mesh,
        in_specs=placed,
        out_specs=(
            P(("row", "col"), None),
            P("row", "col", None),
            P("col", "row", None),
            P("row", "col", None, None),
            P("row", "col", None, None),
        ),
        check_vma=False,
    )
```

```python
import functools

import jax
import jax.numpy as jnp
import numpy as np
from jax import lax
from jax.experimental import pallas as pl
from jax.experimental.pallas import tpu as pltpu
from jax.sharding import PartitionSpec as P

F32 = jnp.float32
BF16 = jnp.bfloat16
SIZE = 2048
PANEL = 256
COUNT = SIZE // PANEL
HALF = PANEL // 2
RANK = 64
NT = (((1,), (1,)), ((), ()))
TN = (((0,), (0,)), ((), ()))
NN = (((1,), (0,)), ((), ()))
EARLY = 2
LANES = COUNT * 4


def tile_start(k, first):
    return sum(COUNT - j for j in range(first, k))


def exact(left, right, dims):
    return lax.dot_general(left, right, dims, precision=lax.Precision.HIGHEST, preferred_element_type=F32)


def split(value):
    high = value.astype(BF16)
    return high, (value - high.astype(F32)).astype(BF16)


def iota(shape, dim):
    return lax.broadcasted_iota(jnp.int32, shape, dim)


def along_rows(value, row):
    return jnp.broadcast_to(value[row : row + 1, :], value.shape)


def along_lanes(value, lane):
    return jnp.broadcast_to(value[:, lane : lane + 1], value.shape)


def total(terms):
    while len(terms) > 1:
        terms = [
            terms[i] + terms[i + 1] if i + 1 < len(terms) else terms[i]
            for i in range(0, len(terms), 2)
        ]
    return terms[0]


def factor_block(block, beside, groups=2):
    count = len(block)
    size = 8 * count
    width = 8 * groups
    work = list(block)
    sub = iota((8, size), 0)
    lane = iota((8, size), 1)
    side = [jnp.where(sub + 8 * i == lane, 1.0, 0.0).astype(F32) for i in range(count)]
    upper = [None] * count
    inverse = [None] * count
    for top in range(0, count, groups):
        beside(top // groups)
        rows = work[top : top + groups]
        eyes = side[top : top + groups]
        near = range(top + groups, min(count, top + 2 * groups))
        cols = [[along_lanes(rows[a], 8 * top + k) for a in range(groups)] for k in range(width)]
        below = {i: [along_lanes(work[i], 8 * top + k) for k in range(width)] for i in near}
        raw = jnp.concatenate(rows, axis=0)
        up = [jnp.zeros((8, size), F32)] * groups
        inv = [jnp.zeros((8, size), F32)] * groups
        pivot = along_rows(cols[0][0], 0)
        for k in range(width):
            ka, ks = divmod(k, 8)
            scale = 1.0 / pivot
            root = lax.rsqrt(pivot)
            here = sub == ks
            heads = {m: along_rows(cols[m][ka], ks) for m in range(k + 1, width)}
            if k + 1 < width:
                na, ns = divmod(k + 1, 8)
                pivot = along_rows(cols[k + 1][na] - (cols[k][na] * heads[k + 1]) * scale, ns)
            row_k = along_rows(rows[ka], ks)
            eye_k = along_rows(eyes[ka], ks)
            up[ka] = jnp.where(here, row_k * root, up[ka])
            inv[ka] = jnp.where(here, eye_k * root, inv[ka])
            times = []
            for a in range(groups):
                ratio = cols[k][a] * scale
                times.append(jnp.where(here, 1.0 - scale, ratio) if a == ka else ratio)
            for a in range(groups):
                rows[a] = rows[a] - times[a] * row_k
                eyes[a] = eyes[a] - times[a] * eye_k
            for m in range(k + 1, width):
                cols[m] = [cols[m][a] - times[a] * heads[m] for a in range(groups)]
        upper[top : top + groups] = up
        inverse[top : top + groups] = inv
        row_all = [along_rows(rows[k // 8], k % 8) for k in range(width)]
        eye_all = [along_rows(eyes[k // 8], k % 8) for k in range(width)]
        for i in near:
            work[i] = work[i] - total([below[i][k] * row_all[k] for k in range(width)])
            side[i] = side[i] - total([below[i][k] * eye_all[k] for k in range(width)])
        if top + 2 * groups < count:
            both = [jnp.concatenate(rows, axis=0), jnp.concatenate(eyes, axis=0)]
            raw_high, raw_low = split(raw)
            high, low = split(jnp.concatenate(both, axis=1))
            change = lax.dot_general(
                jnp.concatenate([raw_high, raw_low, raw_high], axis=0),
                jnp.concatenate([high, high, low], axis=0),
                TN,
                preferred_element_type=F32,
            )
            for i in range(top + 2 * groups, count):
                work[i] = work[i] - change[8 * i : 8 * i + 8, :size]
                side[i] = side[i] - change[8 * i : 8 * i + 8, size:]
    upper = [jnp.where(sub + 8 * i <= lane, upper[i], 0.0) for i in range(count)]
    inverse = [jnp.where(sub + 8 * i >= lane, inverse[i], 0.0) for i in range(count)]
    return jnp.concatenate(upper, axis=0), jnp.concatenate(inverse, axis=0)


def factor_values(value, beside):
    return factor_block([value[8 * i : 8 * i + 8, :] for i in range(value.shape[0] // 8)], beside)


def dot3(left_high, left_low, right_high, right_low):
    left = jnp.concatenate([left_high, left_low, left_high], axis=1)
    right = jnp.concatenate([right_high, right_high, right_low], axis=1)
    return lax.dot_general(left, right, NT, preferred_element_type=F32)


def start_fetch(place_ref, mine_ref, other_ref, work, sems, first, last):
    x0, y0, core = place_ref[2], place_ref[3], place_ref[4]
    for k in range(first, last):
        at = tile_start(k, first)
        for source, owner in ((mine_ref, core), (other_ref, 1 - core)):
            for outer in range(4):
                for inner in range(4):
                    dx = jnp.where(owner == 0, outer, inner)
                    dy = jnp.where(owner == 0, inner, outer)
                    group = (lax.rem(x0 - dx + 4, 4) * 4 + lax.rem(y0 - dy + 4, 4)) * 2 + owner
                    pltpu.make_async_copy(
                        source.at[outer, inner, pl.ds(at, COUNT - k)],
                        work.at[k - first, pl.ds(k, COUNT - k), group],
                        sems.at[k - first],
                    ).start()


def wait_fetch(k, work, sems, first, last):
    for j in range(first, last):

        @pl.when(k == j)
        def _():
            whole = work.at[j - first, pl.ds(j, COUNT - j)]
            pltpu.make_async_copy(whole, whole, sems.at[j - first]).wait()


SOLVES = 5
UPDATES = 18
STEPS = 2 * (HALF // 16)


def plan(first, last, rows):
    spare = last - first
    left = {(p, i, m) for p in range(first, last) for i in range(p, rows) for m in range(p)}
    left -= {(first, first, m) for m in range(first)} | {(p, p, p - 1) for p in range(first, last)}
    table = []
    for k in range(first, last):
        solves = [(k - 1 - first, i, k - 1) for i in range(k + 1, rows)] if k > first else []
        ready = [t for t in left if t[2] < k and t[0] <= k + 1]
        due = lambda t: (t[0] - (t[0] == t[1]), t)
        taken = sorted(ready, key=due)[:UPDATES]
        left -= set(taken)
        assert len(solves) <= SOLVES and all(due(t)[0] > k for t in left)
        updates = [(p - first, p, i, m) for p, i, m in taken]
        solves += [(spare, 0, COUNT)] * (SOLVES - len(solves))
        updates += [(spare, k, k, 0)] * (UPDATES - len(updates))
        table.append([x for t in solves + updates for x in t])
    assert not left
    return np.array(table, np.int32)


def factor_panel(tile, store, inverse, beside):
    first_up, first_inv = factor_values(tile[:HALF, :HALF], beside)
    cross = exact(tile[HALF:, :HALF], first_inv, NT)
    rest = tile[HALF:, HALF:] - exact(cross, cross, NT)
    steps = HALF // 16
    second_up, second_inv = factor_values(rest, lambda j: beside(j + steps))
    corner = -exact(second_inv, exact(cross, first_inv, NN), NN)
    zero = jnp.zeros((HALF, HALF), F32)
    inv_top = jnp.concatenate([first_inv, zero], axis=1)
    inv_bottom = jnp.concatenate([corner, second_inv], axis=1)
    inverse[0], inverse[1] = split(jnp.concatenate([inv_top, inv_bottom], axis=0))
    top = jnp.concatenate([first_up.T, zero], axis=1)
    bottom = jnp.concatenate([cross, second_up.T], axis=1)
    store(jnp.concatenate([top, bottom], axis=0))


def factor_range(plan_ref, work, high, low, inverses, wait, first, last):
    def solve(slot, i, k, to):
        value = dot3(*split(work[slot, i].reshape(PANEL, PANEL)), inverses[k, 0], inverses[k, 1])
        work[slot, i] = value.reshape(LANES, 8, PANEL)
        top, bottom = split(value)
        high[to, i] = top
        low[to, i] = bottom

    def update(slot, k, i, m):
        value = dot3(high[m, i], low[m, i], high[m, k], low[m, k]).reshape(LANES, 8, PANEL)
        work[slot, i] = work[slot, i] - value

    def step(k, at, items):
        def beside(j):
            share = lambda x: -(-x * len(items) // STEPS)
            for item in items[share(j) : share(j + 1)]:
                item()

        def store(value):
            work[at, k] = value.reshape(LANES, 8, PANEL)

        factor_panel(work[at, k].reshape(PANEL, PANEL), store, inverses.at[k], beside)

    def head(k, at):
        solve(at - 1, k, k - 1, k - 1)
        update(at, k, k, k - 1)

    def early():
        for k in range(first, last):
            wait(jnp.int32(k))
            items = []
            if k > first:
                head(k, k)
                items = [functools.partial(solve, k - 1, i, k - 1, k - 1) for i in range(k + 1, COUNT)]
                items += [functools.partial(update, k, k, i, k - 1) for i in range(k + 1, COUNT)]
            step(k, k, items)

    def late_step_of(k, carry):
        at = k - first
        wait(k + 1)

        @pl.when(k > first)
        def _():
            head(k, at)

        def item(j):
            if j < SOLVES:
                slot, i, to = (plan_ref[at, 3 * j + x] for x in range(3))
                solve(slot, i, jnp.maximum(k - 1, first), to)
            else:
                base = 3 * SOLVES + 4 * (j - SOLVES)
                update(*(plan_ref[at, base + x] for x in range(4)))

        step(k, at, [functools.partial(item, j) for j in range(SOLVES + UPDATES)])
        return carry

    if plan_ref is None:
        early()
    else:
        wait(jnp.int32(first))
        for m in range(first):
            update(0, first, first, m)
        lax.fori_loop(first, last, late_step_of, 0)
    return solve


def own_rows(place_ref, own_ref, work, first, last):
    own_tile, own_group = place_ref[0], place_ref[1]
    for k in range(first, last):
        mine = work[k - first, own_tile, own_group]
        own_ref[:, k * PANEL : (k + 1) * PANEL] = jnp.where(own_tile >= k, mine, 0.0)


def early_kernel(place_ref, mine_ref, other_ref, own_ref, high, low, inverse_ref, work, sems):
    start_fetch(place_ref, mine_ref, other_ref, work, sems, 0, EARLY)
    wait = lambda k: wait_fetch(k, work, sems, 0, EARLY)
    solve = factor_range(None, work, high, low, inverse_ref, wait, 0, EARLY)
    last = EARLY - 1
    for i in range(EARLY, COUNT):
        solve(last, i, last, last)
    own_rows(place_ref, own_ref, work, 0, EARLY)


def late_kernel(
    place_ref, plan_ref, mine_ref, other_ref, high_ref, low_ref, inverse_ref, early_ref, cols_ref, cols_other_ref, trail_u_ref, trail_v_ref,
    own_ref, row_ref, col_ref, grown_u_ref, grown_v_ref,
    work, high, low, inverses, rows_all, pan, base, solved, change, sems, more_sems,
):
    x0, y0, core = place_ref[2], place_ref[3], place_ref[4]
    last = COUNT - 1
    loads = []
    for j in range(EARLY):
        loads.append(pltpu.make_async_copy(high_ref.at[j], high.at[j, pl.ds(0, COUNT)], more_sems.at[3 * j]))
        loads.append(pltpu.make_async_copy(low_ref.at[j], low.at[j, pl.ds(0, COUNT)], more_sems.at[3 * j + 1]))
        loads.append(pltpu.make_async_copy(inverse_ref.at[j], inverses.at[j], more_sems.at[3 * j + 2]))
    for copy in loads:
        copy.start()
    tiles = tile_start(COUNT, EARLY)
    row_sem = more_sems.at[3 * EARLY + 1]
    for source, owner in ((mine_ref, core), (other_ref, 1 - core)):
        for outer in range(4):
            for inner in range(4):
                dx = jnp.where(owner == 0, outer, inner)
                dy = jnp.where(owner == 0, inner, outer)
                group = (lax.rem(x0 - dx + 4, 4) * 4 + lax.rem(y0 - dy + 4, 4)) * 2 + owner
                pltpu.make_async_copy(source.at[outer, inner, pl.ds(tiles, 4)], rows_all.at[:, group], row_sem).start()
    start_fetch(place_ref, mine_ref, other_ref, work, sems, EARLY, COUNT)
    column_pieces = []
    for source, first_bit in ((cols_ref, 0), (cols_other_ref, 1)):
        for second in range(2):
            for third in range(2):
                place = (place_ref[0] ^ (4 * third + 2 * second + first_bit)) * 8
                column_pieces.append((source.at[second, third], pl.multiple_of(place, 8)))
    col_sem, out_sem = more_sems.at[3 * EARLY], more_sems.at[3 * EARLY + 4]
    for source, place in column_pieces:
        pltpu.make_async_copy(source.at[1], pan.at[pl.ds(RANK + place, 8)], col_sem).start()
        pltpu.make_async_copy(source.at[0], grown_v_ref.at[pl.ds(RANK + place, 8)], out_sem).start()
    passing = [
        pltpu.make_async_copy(trail_u_ref, grown_u_ref.at[pl.ds(0, RANK)], more_sems.at[3 * EARLY + 2]),
        pltpu.make_async_copy(trail_v_ref, grown_v_ref.at[pl.ds(0, RANK)], more_sems.at[3 * EARLY + 3]),
    ]
    for copy in passing:
        copy.start()
    for copy in loads:
        copy.wait()
    pltpu.make_async_copy(rows_all, rows_all, row_sem).wait()
    pltpu.make_async_copy(pan.at[pl.ds(RANK, RANK)], pan.at[pl.ds(RANK, RANK)], col_sem).wait()
    for k in range(COUNT):
        cols = slice(k * PANEL, (k + 1) * PANEL)
        for r in range(2):
            base[32 * r : 32 * r + 32, cols] = rows_all[r, :, k, :]
            pan[32 * r : 32 * r + 32, cols] = rows_all[2 + r, :, k, :]
    empty = jnp.zeros((LANES // 2, 8, PANEL), F32)
    nothing = jnp.zeros((HALF, PANEL), BF16)
    for k in range(COUNT):
        cols = slice(k * PANEL, (k + 1) * PANEL)
        value = pan[:, cols]
        if k < EARLY:
            for m in range(k):
                value = value - dot3(high[m, COUNT, :HALF], low[m, COUNT, :HALF], high[m, k], low[m, k])
            value = dot3(*split(value), inverses[k, 0], inverses[k, 1])
            solved[:, cols] = value
            high[k, COUNT, :HALF], low[k, COUNT, :HALF] = split(value)
            high[k, COUNT, HALF:] = nothing
            low[k, COUNT, HALF:] = nothing
        else:
            work[k - EARLY, COUNT, : LANES // 2] = value.reshape(LANES // 2, 8, PANEL)
            work[k - EARLY, COUNT, LANES // 2 :] = empty
    wait = lambda k: wait_fetch(k, work, sems, EARLY, COUNT)
    solve = factor_range(plan_ref, work, high, low, inverses, wait, EARLY, COUNT)
    solve(last - EARLY, COUNT, last, last)
    for k in range(EARLY, COUNT):
        solved[:, k * PANEL : (k + 1) * PANEL] = work[k - EARLY, COUNT, : LANES // 2].reshape(HALF, PANEL)
    coupling = exact(solved[:RANK, :], solved[RANK:, :], NT)
    change[...] = -exact(coupling, base[...], TN)
    out = pltpu.make_async_copy(change, grown_u_ref.at[pl.ds(RANK, RANK)], more_sems.at[3 * EARLY + 5])
    out.start()
    own_ref[:, : EARLY * PANEL] = early_ref[...]
    own_rows(place_ref, own_ref, work, EARLY, COUNT)
    for r in range(2):
        row_ref[r : r + 1, :] = solved[pl.ds(32 * r + place_ref[1], 1), :]
    col_ref[...] = solved[pl.ds(pl.multiple_of(RANK + place_ref[0] * 8, 8), 8), :]
    for copy in passing:
        copy.wait()
    whole = grown_v_ref.at[pl.ds(RANK, RANK)]
    pltpu.make_async_copy(whole, whole, out_sem).wait()
    out.wait()


VMEM = pl.BlockSpec(memory_space=pltpu.VMEM)
SMEM = pl.BlockSpec(memory_space=pltpu.SMEM)
ANYWHERE = pl.BlockSpec(memory_space=pl.ANY)
ROOM = pltpu.CompilerParams(vmem_limit_bytes=60 * 1024 * 1024)


def early_step(place, mine, other):
    return pl.pallas_call(
        early_kernel,
        out_shape=(
            jax.ShapeDtypeStruct((8, EARLY * PANEL), F32),
            jax.ShapeDtypeStruct((EARLY, COUNT, PANEL, PANEL), BF16),
            jax.ShapeDtypeStruct((EARLY, COUNT, PANEL, PANEL), BF16),
            jax.ShapeDtypeStruct((EARLY, 2, PANEL, PANEL), BF16),
        ),
        in_specs=[SMEM, ANYWHERE, ANYWHERE],
        out_specs=(VMEM, VMEM, VMEM, VMEM),
        scratch_shapes=[
            pltpu.VMEM((EARLY, COUNT, LANES, 8, PANEL), F32),
            pltpu.SemaphoreType.DMA((EARLY,)),
        ],
        compiler_params=ROOM,
        cost_estimate=pl.CostEstimate(flops=30 * 10**9, bytes_accessed=80 * 10**6, transcendentals=0),
    )(place, mine, other)


def late_step(place, mine, other, high, low, inverse, early, cols, cols_other, trail_u, trail_v):
    late = COUNT - EARLY
    return pl.pallas_call(
        late_kernel,
        out_shape=(
            jax.ShapeDtypeStruct((8, SIZE), F32),
            jax.ShapeDtypeStruct((2, SIZE), F32),
            jax.ShapeDtypeStruct((8, SIZE), F32),
            jax.ShapeDtypeStruct((2 * RANK, SIZE), F32),
            jax.ShapeDtypeStruct((2 * RANK, SIZE), F32),
        ),
        in_specs=[SMEM, SMEM] + [ANYWHERE] * 5 + [VMEM] + [ANYWHERE] * 4,
        out_specs=(VMEM, VMEM, VMEM, ANYWHERE, ANYWHERE),
        scratch_shapes=[
            pltpu.VMEM((late + 1, COUNT + 1, LANES, 8, PANEL), F32),
            pltpu.VMEM((COUNT + 1, COUNT + 1, PANEL, PANEL), BF16),
            pltpu.VMEM((COUNT + 1, COUNT + 1, PANEL, PANEL), BF16),
            pltpu.VMEM((COUNT, 2, PANEL, PANEL), BF16),
            pltpu.VMEM((4, 32, 8, PANEL), F32),
            pltpu.VMEM((2 * RANK, SIZE), F32),
            pltpu.VMEM((RANK, SIZE), F32),
            pltpu.VMEM((2 * RANK, SIZE), F32),
            pltpu.VMEM((RANK, SIZE), F32),
            pltpu.SemaphoreType.DMA((late,)),
            pltpu.SemaphoreType.DMA((3 * EARLY + 6,)),
        ],
        compiler_params=ROOM,
        cost_estimate=pl.CostEstimate(flops=80 * 10**9, bytes_accessed=300 * 10**6, transcendentals=0),
    )(place, jnp.asarray(plan(EARLY, COUNT, COUNT + 1)), mine, other, high, low, inverse, early, cols, cols_other, trail_u, trail_v)


def column(x, y, core):
    return (x % 4 * 4 + y % 4) * 2 + core


def ring(shift, stage):
    pairs = []
    for x in range(4):
        for y in range(4):
            for core in range(2):
                along_y = stage == core
                target = column(x, y + shift, core) if along_y else column(x + shift, y, core)
                pairs.append((column(x, y, core), target))
    return pairs


def spread_parts(piece, stage):
    return [piece] + [lax.ppermute(piece, "col", ring(s, stage)) for s in (1, 2, 3)]


def spread(piece, stage):
    return jnp.stack(spread_parts(piece, stage))


def tiles_of(bands, first, last):
    return jnp.concatenate([bands[k, k:] for k in range(first, last)], axis=0)


def swap(piece):
    return lax.ppermute(piece, "col", [(i, i ^ 1) for i in range(32)])


def across(piece, bit):
    return lax.ppermute(piece, "row", [(i, i ^ bit) for i in range(8)])


def body(diag_tile, row_pan_u, row_pan_v, col_pan_u, col_pan_v, trail_u, trail_v):
    row = lax.axis_index("row")
    col = lax.axis_index("col")
    copies = jnp.broadcast_to(diag_tile[None], (COUNT, 8, SIZE))
    bands = lax.all_to_all(copies, "row", 0, 0)
    bands = bands.reshape(COUNT, 8, COUNT, PANEL).transpose(2, 0, 1, 3)
    rows = jnp.concatenate([row_pan_u[0], row_pan_v[0]], axis=0).reshape(4, COUNT, PANEL)
    count = tile_start(EARLY, 0)
    tiles = jnp.concatenate([tiles_of(bands, 0, EARLY), tiles_of(bands, EARLY, COUNT), rows], axis=0)
    cols = lax.optimization_barrier((jnp.stack([col_pan_u[0], col_pan_v[0]]), bands))[0]
    cols = jnp.stack([cols, across(cols, 4)])
    tiles = spread_parts(tiles, 0)
    tiles, cols = lax.optimization_barrier((tiles, cols))
    cols = jnp.stack([cols, across(cols, 2)])
    early = spread(jnp.stack([part[:count] for part in tiles]), 1)
    early, cols = lax.optimization_barrier((early, cols))
    early_other = swap(early)
    cols_other = across(cols, 1)
    early, tiles = lax.optimization_barrier((early, tiles))
    late = spread_parts(jnp.stack([part[count:] for part in tiles]), 1)
    place = jnp.stack([row, col, col // 8, col // 2 % 4, col % 2]).astype(jnp.int32)
    own, high, low, inverse = early_step(place, early, early_other)
    late, cols_other, high = lax.optimization_barrier((late, cols_other, high))
    late = jnp.stack(late)
    late_other = swap(late)
    own, row_own, col_own, grown_u, grown_v = late_step(
        place, late, late_other, high, low, inverse, own, cols, cols_other, trail_u[0, 0], trail_v[0, 0]
    )
    return (own, row_own[None], col_own[None], grown_u[None, None], grown_v[None, None])


def solution(mesh):
    placed = (
        P(("row", "col"), None),
        P("row", "col", None),
        P("row", "col", None),
        P("col", "row", None),
        P("col", "row", None),
        P("row", "col", None, None),
        P("row", "col", None, None),
    )
    return jax.shard_map(
        body,
        mesh=mesh,
        in_specs=placed,
        out_specs=(
            P(("row", "col"), None),
            P("row", "col", None),
            P("col", "row", None),
            P("row", "col", None, None),
            P("row", "col", None, None),
        ),
        check_vma=False,
    )
```
